256 devices in a mesh: rows: 32 (over z, x), sub: 8 (over y, core).
Axes of the slice: x: 4, y: 4, z: 8, core: 2. Of those that a mesh axis runs over, the one named last changes fastest.
Arguments:
- snapshots: float32 [262144, 1024], P(('rows', 'sub')), may hold values from -33 to 33
- range_test: float32 [1024, 256], replicated, may hold values from -0.1875 to 0.1875
- corange_test: float32 [512, 262144], P(None, ('rows', 'sub')), may hold values from -0.01171875 to 0.01171875
Outputs:
- basis: float32 [262144, 256], P(('rows', 'sub'))
- corange: float32 [512, 1024], replicated
- core: float32 [256, 512], replicated
The draws below stay inside these ranges and needn't reach their ends.
All inputs are finite; a program needn't handle non-finite values.
Results may differ from the reference program's by a relative error of at most 0.0003.
Values sent between devices are 32-bit elements; how exact they have to be, the bound alone decides.
No kernel may reach another device: no remote copies, remote signals or barrier semaphores. Data moves between devices by JAX's collectives and lax.ppermute only.
A program may use at most 128 MiB of HBM per device.

```python
import math
import jax
import jax.numpy as jnp
from jax import lax

SNAPS = 1024
RANK = 256
CORANGE = 512
ROWS = 262144


def draw_snapshots(key, part):
    key = jax.random.fold_in(key, 11)
    keys = jax.random.split(key, 3)
    terms = 8
    row_factors = jax.random.truncated_normal(keys[0], -3.0, 3.0, (terms, ROWS), jnp.float32)
    col_factors = jax.random.truncated_normal(keys[1], -3.0, 3.0, (terms, SNAPS), jnp.float32)
    noise = jax.random.truncated_normal(keys[2], -3.0, 3.0, (ROWS, SNAPS), jnp.float32)
    floor = math.sqrt(RANK) / 600.0
    field = noise * floor
    amplitude = 1.0
    for index in range(terms):
        field = field + amplitude * row_factors[index][:, None] * col_factors[index][None, :]
        amplitude = amplitude * 0.6
    return field.astype(jnp.float32)


def block_levels(rng, extent, cuts, least, largest):
    loudness, own = 1.0, jax.random.fold_in(rng, 6)
    for axis_at, shards_of in cuts:
        draws = jnp.exp(jax.random.uniform(jax.random.fold_in(own, axis_at), (shards_of,), jnp.float32, least / len(cuts), largest / len(cuts)))
        loudness = loudness * jnp.repeat(draws, extent[axis_at] // shards_of).reshape([-1 if axis == axis_at else 1 for axis in range(len(extent))])
    return loudness


def gaussian(rng, extent, deviation, limit, cuts=(), dtype=jnp.bfloat16):
    drawn = deviation * jax.random.normal(rng, extent, jnp.float32)
    if cuts:
        drawn = drawn * block_levels(rng, extent, cuts, -0.22, 0.18)
    return jnp.clip(drawn, -limit, limit).astype(dtype)


def setup_inputs(seed: int = 0) -> dict:
    streams_of = jax.random.split(jax.random.key(seed), 4)
    snapshots = draw_snapshots(jax.random.fold_in(streams_of[3], 71), 0)
    range_test = gaussian(streams_of[1], (SNAPS, RANK), SNAPS ** -0.5, 0.1875, (), jnp.float32)
    corange_test = gaussian(streams_of[2], (CORANGE, ROWS), ROWS ** -0.5, 0.01171875, ((1, 256),), jnp.float32)
    return dict(snapshots=snapshots, range_test=range_test, corange_test=corange_test)


def lower_factor(block):
    gram = jnp.einsum('rk,rj->kj', block, block, precision=lax.Precision.HIGHEST) / ROWS
    return jnp.linalg.cholesky(gram)

def right_solve(factor, block):
    return lax.linalg.triangular_solve(factor, block, left_side=False, lower=True, transpose_a=True)

def reference(snapshots, range_test, corange_test):
    sketch = jnp.dot(snapshots, range_test, precision=lax.Precision.HIGHEST)
    corange = jnp.dot(corange_test, snapshots, precision=lax.Precision.HIGHEST)
    first = lower_factor(sketch)
    basis_one = right_solve(first, sketch)
    second = lower_factor(basis_one)
    basis = right_solve(second, basis_one)
    core = jnp.einsum('rk,lr->kl', basis, corange_test, precision=lax.Precision.HIGHEST)
    return (basis, corange, core)
```

```python
import jax
import jax.numpy as jnp
from jax import lax
from jax.sharding import Mesh, PartitionSpec as P

HIGHEST = lax.Precision.HIGHEST
SIZES = {"z": 8, "x": 4, "y": 4, "core": 2}


def swap(value, axis, mask):
    return lax.ppermute(value, axis, [(i, i ^ mask) for i in range(SIZES[axis])])


def halve(value, axis, mask, upper):
    half = value.shape[0] // 2
    sent = lax.dynamic_slice_in_dim(value, jnp.where(upper, 0, half), half)
    kept = lax.dynamic_slice_in_dim(value, jnp.where(upper, half, 0), half)
    return kept + swap(sent, axis, mask)


def double(value, axis, mask):
    return value + swap(value, axis, mask)


def join(value, axis, mask, upper):
    other = swap(value, axis, mask)
    return jnp.concatenate([jnp.where(upper, other, value), jnp.where(upper, value, other)])


def all_sum(value):
    core = lax.axis_index("core") == 1
    y = lax.axis_index("y")
    low, high = y % 2 == 1, y >= 2
    value = halve(value, "core", 1, core)
    value = halve(value, "y", 1, low)
    value = halve(value, "y", 2, high)
    for axis, masks in (("x", (1, 3)), ("z", (1, 3, 7))):
        for mask in masks:
            value = double(value, axis, mask)
    value = join(value, "y", 2, high)
    value = join(value, "y", 1, low)
    return join(value, "core", 1, core)


def gram_term(block, total):
    return jnp.einsum("rk,rj->kj", block, block, precision=HIGHEST) / total


def right_solve(factor, block):
    return lax.linalg.triangular_solve(factor, block, left_side=False, lower=True, transpose_a=True)


def shards(snapshots, range_test, corange_test):
    total = snapshots.shape[0] * 256
    sketch = jnp.dot(snapshots, range_test, precision=HIGHEST)
    gram_one = all_sum(gram_term(sketch, total))
    corange = all_sum(jnp.dot(corange_test, snapshots, precision=HIGHEST))
    crossed = jnp.dot(corange, range_test, precision=HIGHEST)
    first = jnp.linalg.cholesky(gram_one)
    rows = sketch.shape[0]
    both = right_solve(first, jnp.concatenate([sketch, crossed]))
    second = jnp.linalg.cholesky(all_sum(gram_term(both[:rows], total)))
    both = right_solve(second, both)
    return both[:rows], corange, both[rows:].T


def solution(mesh):
    fine = Mesh(mesh.devices.reshape(8, 4, 4, 2), ("z", "x", "y", "core"))
    rows = ("z", "x", "y", "core")
    in_specs = (P(rows, None), P(), P(None, rows))
    out_specs = (P(rows, None), P(), P())
    return jax.shard_map(shards, mesh=fine, in_specs=in_specs, out_specs=out_specs, check_vma=False)
```

```python
import itertools

import jax
import jax.numpy as jnp
from jax import lax
from jax.experimental import pallas as pl
from jax.experimental.pallas import tpu as pltpu
from jax.sharding import Mesh, PartitionSpec as P

HIGHEST = lax.Precision.HIGHEST
F32, BF16 = jnp.float32, jnp.bfloat16


def mul(a, b):
    return lax.dot_general(a, b, (((1,), (0,)), ((), ())), precision=HIGHEST, preferred_element_type=F32)


def mul_t(a, b):
    return lax.dot_general(a, b, (((1,), (1,)), ((), ())), precision=HIGHEST, preferred_element_type=F32)


def factor(work, unit, upper, inverse):
    unit[...] = jnp.where(eye(128), 1.0, 0.0)
    for p in range(16):
        rows = pl.ds(8 * p, 8)
        panel, tail = work[rows, :], unit[rows, :]
        column = [jnp.broadcast_to(panel[:, 8 * p + j : 8 * p + j + 1], (8, 128)) for j in range(8)]
        s = [[column[j][i : i + 1, :] if j >= i else None for j in range(8)] for i in range(8)]
        r = [panel[i : i + 1, :] for i in range(8)]
        t = [tail[i : i + 1, :] for i in range(8)]
        inv = [None] * 8
        for j in range(8):
            inv[j] = 1.0 / s[j][j]
            for i in range(j + 1, 8):
                m = s[j][i] * inv[j]
                for k in range(i, 8):
                    s[i][k] = s[i][k] - m * s[j][k]
                r[i] = r[i] - m * r[j]
                t[i] = t[i] - m * t[j]
        for q in range(p + 1, 16):
            below = pl.ds(8 * q, 8)
            a, b = work[below, :], unit[below, :]
            c = [jnp.broadcast_to(a[:, 8 * p + j : 8 * p + j + 1], (8, 128)) for j in range(8)]
            for j in range(8):
                f = c[j] * inv[j]
                for k in range(j + 1, 8):
                    c[k] = c[k] - f * s[j][k]
                a = a - f * r[j]
                b = b - f * t[j]
            work[below, :] = a
            unit[below, :] = b
        root = [lax.rsqrt(s[i][i]) for i in range(8)]
        lane = lax.broadcasted_iota(jnp.int32, (1, 128), 1)
        upper[rows, :] = jnp.concatenate([jnp.where(lane >= 8 * p + i, r[i] * root[i], 0.0) for i in range(8)])
        inverse[rows, :] = jnp.concatenate([t[i] * root[i] for i in range(8)])


def eye(n):
    return lax.broadcasted_iota(jnp.int32, (n, n), 0) == lax.broadcasted_iota(jnp.int32, (n, n), 1)


def slices(value, axis):
    big = jnp.max(jnp.abs(value), axis=axis, keepdims=True) * 131072.0
    h = (value + big) - big
    m = value - h
    m1 = m.astype(BF16)
    m = m - m1.astype(F32)
    m2 = m.astype(BF16)
    m3 = (m - m2.astype(F32)).astype(BF16)
    return h.astype(BF16), m1, m2, m3


def blocked(gram, upper, inverse, work, unit, u, x):
    work[...] = gram[:128, :128]
    factor(work, unit, u, x)
    x00 = x[...]
    u01 = mul(x00, gram[:128, 128:])
    upper[:128, :128] = u[...]
    upper[:128, 128:] = u01
    upper[128:, :128] = jnp.zeros((128, 128), F32)
    inverse[:128, :128] = x00
    inverse[:128, 128:] = jnp.zeros((128, 128), F32)
    l10 = u01.T
    work[...] = gram[128:, 128:] - mul(l10, u01)
    factor(work, unit, u, x)
    x11 = x[...]
    upper[128:, 128:] = u[...]
    inverse[128:, 128:] = x11
    inverse[128:, :128] = -mul(x11, mul(l10, x00))


def bf(a, b):
    return lax.dot_general(a, b, (((1,), (0,)), ((), ())), preferred_element_type=F32)


def low(e):
    row = lax.broadcasted_iota(jnp.int32, e.shape, 0)
    col = lax.broadcasted_iota(jnp.int32, e.shape, 1)
    return jnp.where(row > col, e, jnp.where(row == col, 0.5 * e, 0.0))


def chol_kernel(gram, rest, out, upper, inverse, work, unit, u, x, second):
    blocked(gram, upper, inverse, work, unit, u, x)
    up = upper[...]
    lo = up.T
    uh, u1, u2, u3 = slices(up, 0)
    lh, l1, l2, l3 = slices(lo, 1)
    left = jnp.concatenate([l2, l1, l1, l3, lh, l2, lh, l1, lh], axis=1)
    right = jnp.concatenate([u1, u2, u1, uh, u3, uh, u2, uh, u1], axis=0)
    resid = ((gram[...] - bf(lh, uh)) - bf(left, right)) + rest[...]
    first = inverse[...]
    one = jnp.where(eye(256), 1.0, 0.0)
    gap = mul(first, lo) - one
    e = mul_t(mul(first, resid), first) + mul_t(gap, gap)
    e = 0.5 * (e + e.T) + (gap + gap.T)
    second[...] = one + e
    size = jnp.sqrt(jnp.sum(e * e))

    @pl.when(size < 0.25)
    def _():
        y = one - low(e)
        for _ in range(2):
            f = mul_t(mul(y, e), y) + (mul_t(y, y) - one)
            y = y - mul(low(f), y)
        out[...] = mul(y, first)

    @pl.when(jnp.logical_not(size < 0.25))
    def _():
        blocked(second, upper, inverse, work, unit, u, x)
        out[...] = mul(inverse[...], first)


def chol(gram, rest):
    big, small = pltpu.VMEM((256, 256), F32), pltpu.VMEM((128, 128), F32)
    return pl.pallas_call(
        chol_kernel,
        out_shape=jax.ShapeDtypeStruct((256, 256), F32),
        in_specs=[pl.BlockSpec(memory_space=pltpu.VMEM)] * 2,
        out_specs=pl.BlockSpec(memory_space=pltpu.VMEM),
        scratch_shapes=[big, big, small, small, small, small, big],
        compiler_params=pltpu.CompilerParams(vmem_limit_bytes=32 << 20),
    )(gram, rest)


AXES = ("z", "x", "y", "core")


def pairs(change):
    def index(z, x, y, c):
        return ((z * 4 + x) * 4 + y) * 2 + c
    places = itertools.product(range(8), range(4), range(4), range(2))
    return [(index(*place), index(*change(*place))) for place in places]


CORE = pairs(lambda z, x, y, c: (z, x, y, c ^ 1))
A1 = pairs(lambda z, x, y, c: (z, x ^ 1, y, c) if c else (z, x, y ^ 1, c))
A2 = pairs(lambda z, x, y, c: (z, x ^ 3, y, c) if c else (z, x, y ^ 3, c))
B1 = pairs(lambda z, x, y, c: (z, x, y ^ 1, c) if c else (z, x ^ 1, y, c))
B2 = pairs(lambda z, x, y, c: (z, x, y ^ 3, c) if c else (z, x ^ 3, y, c))
Z1, Z2, Z3 = (pairs(lambda z, x, y, c, m=m: (z ^ m, x, y, c)) for m in (1, 3, 7))


def swap(value, perm):
    return lax.ppermute(value, AXES, perm)


def halve(value, perm, upper):
    half = value.shape[0] // 2
    sent = lax.dynamic_slice_in_dim(value, jnp.where(upper, 0, half), half)
    kept = lax.dynamic_slice_in_dim(value, jnp.where(upper, half, 0), half)
    return kept + swap(sent, perm)


def join(value, perm, upper):
    other = swap(value, perm)
    return jnp.concatenate([jnp.where(upper, other, value), jnp.where(upper, value, other)])


def place():
    core = lax.axis_index("core") == 1
    x, y = lax.axis_index("x"), lax.axis_index("y")
    a, b = jnp.where(core, x, y), jnp.where(core, y, x)
    return core, (a == 1) | (a == 2), a >= 2, (b == 1) | (b == 2), b >= 2


def double_pair(s, e, perm):
    other = swap(jnp.concatenate([s, e], axis=1), perm)
    n = s.shape[1]
    t, f = other[:, :n], other[:, n:]
    total = s + t
    part = total - s
    return total, ((s - (total - part)) + (t - part)) + (e + f)


def sum_pair(value):
    core, a1, a2, _, _ = place()
    value = halve(value, CORE, core)
    value = halve(value, A1, a1)
    value = halve(value, A2, a2)
    s, e = value, jnp.zeros_like(value)
    for perm in (B1, B2, Z1, Z2, Z3):
        s, e = double_pair(s, e, perm)
    both = jnp.concatenate([s, e], axis=1)
    both = join(both, A2, a2)
    both = join(both, A1, a1)
    both = join(both, CORE, core)
    return both[:, : s.shape[1]], both[:, s.shape[1] :]


def sum_all(value):
    core, a1, a2, b1, b2 = place()
    value = halve(value, CORE, core)
    value = halve(value, A1, a1)
    value = halve(value, A2, a2)
    value = halve(value, B1, b1)
    value = halve(value, B2, b2)
    for perm in (Z1, Z2, Z3):
        value = value + swap(value, perm)
    value = join(value, B2, b2)
    value = join(value, B1, b1)
    value = join(value, A2, a2)
    value = join(value, A1, a1)
    return join(value, CORE, core)


def shards(snapshots, range_test, corange_test):
    total = snapshots.shape[0] * 256
    sketch = jnp.dot(snapshots, range_test, precision=HIGHEST)
    gram_local = jnp.einsum("rk,rj->kj", sketch, sketch, precision=HIGHEST) / total
    gram_local, snapshots = lax.optimization_barrier((gram_local, snapshots))
    gram, rest = sum_pair(gram_local)
    corange = sum_all(jnp.dot(corange_test, snapshots, precision=HIGHEST))
    inverse = chol(gram, rest)
    basis = jnp.einsum("rk,jk->rj", sketch, inverse, precision=HIGHEST)
    crossed = jnp.dot(corange, range_test, precision=HIGHEST)
    core = jnp.einsum("jk,lk->jl", inverse, crossed, precision=HIGHEST)
    return basis, corange, core


def solution(mesh):
    fine = Mesh(mesh.devices.reshape(8, 4, 4, 2), AXES)
    in_specs = (P(AXES, None), P(), P(None, AXES))
    out_specs = (P(AXES, None), P(), P())
    return jax.shard_map(shards, mesh=fine, in_specs=in_specs, out_specs=out_specs, check_vma=False)
```

```python
import functools
import itertools

import jax
import jax.numpy as jnp
from jax import lax
from jax.experimental import pallas as pl
from jax.experimental.pallas import tpu as pltpu
from jax.sharding import Mesh, PartitionSpec as P

HIGHEST = lax.Precision.HIGHEST
F32, BF16 = jnp.float32, jnp.bfloat16


def mul(a, b):
    return lax.dot_general(a, b, (((1,), (0,)), ((), ())), precision=HIGHEST, preferred_element_type=F32)


def mul_t(a, b):
    return lax.dot_general(a, b, (((1,), (1,)), ((), ())), precision=HIGHEST, preferred_element_type=F32)


def factor(work, unit, upper, inverse):
    unit[...] = jnp.where(eye(128), 1.0, 0.0)
    for p in range(16):
        rows = pl.ds(8 * p, 8)
        panel, tail = work[rows, :], unit[rows, :]
        column = [jnp.broadcast_to(panel[:, 8 * p + j : 8 * p + j + 1], (8, 128)) for j in range(8)]
        s = [[column[j][i : i + 1, :] if j >= i else None for j in range(8)] for i in range(8)]
        r = [panel[i : i + 1, :] for i in range(8)]
        t = [tail[i : i + 1, :] for i in range(8)]
        inv = [None] * 8
        for j in range(8):
            inv[j] = 1.0 / s[j][j]
            for i in range(j + 1, 8):
                m = s[j][i] * inv[j]
                for k in range(i, 8):
                    s[i][k] = s[i][k] - m * s[j][k]
                r[i] = r[i] - m * r[j]
                t[i] = t[i] - m * t[j]
        for q in range(p + 1, 16):
            below = pl.ds(8 * q, 8)
            a, b = work[below, :], unit[below, :]
            c = [jnp.broadcast_to(a[:, 8 * p + j : 8 * p + j + 1], (8, 128)) for j in range(8)]
            for j in range(8):
                f = c[j] * inv[j]
                for k in range(j + 1, 8):
                    c[k] = c[k] - f * s[j][k]
                a = a - f * r[j]
                b = b - f * t[j]
            work[below, :] = a
            unit[below, :] = b
        root = [lax.rsqrt(s[i][i]) for i in range(8)]
        lane = lax.broadcasted_iota(jnp.int32, (1, 128), 1)
        upper[rows, :] = jnp.concatenate([jnp.where(lane >= 8 * p + i, r[i] * root[i], 0.0) for i in range(8)])
        inverse[rows, :] = jnp.concatenate([t[i] * root[i] for i in range(8)])


def eye(n):
    return lax.broadcasted_iota(jnp.int32, (n, n), 0) == lax.broadcasted_iota(jnp.int32, (n, n), 1)


def slices(value, axis):
    big = jnp.max(jnp.abs(value), axis=axis, keepdims=True) * 131072.0
    h = (value + big) - big
    m = value - h
    m1 = m.astype(BF16)
    m = m - m1.astype(F32)
    m2 = m.astype(BF16)
    m3 = (m - m2.astype(F32)).astype(BF16)
    return h.astype(BF16), m1, m2, m3


def extend(gram, u00, x00, upper, inverse, work, unit, u, x):
    u01 = mul(x00, gram[:128, 128:])
    upper[:128, :128] = u00
    upper[:128, 128:] = u01
    upper[128:, :128] = jnp.zeros((128, 128), F32)
    inverse[:128, :128] = x00
    inverse[:128, 128:] = jnp.zeros((128, 128), F32)
    l10 = u01.T
    work[...] = gram[128:, 128:] - mul(l10, u01)
    factor(work, unit, u, x)
    x11 = x[...]
    upper[128:, 128:] = u[...]
    inverse[128:, 128:] = x11
    inverse[128:, :128] = -mul(x11, mul(l10, x00))


def bf(a, b):
    return lax.dot_general(a, b, (((1,), (0,)), ((), ())), preferred_element_type=F32)


def low(e):
    row = lax.broadcasted_iota(jnp.int32, e.shape, 0)
    col = lax.broadcasted_iota(jnp.int32, e.shape, 1)
    return jnp.where(row > col, e, jnp.where(row == col, 0.5 * e, 0.0))


def factor_kernel(gram, u, x, work, unit):
    work[...] = gram[:128, :128]
    factor(work, unit, u, x)


def extend_kernel(gram, u00, x00, upper, inverse, work, unit, u, x):
    extend(gram, u00[...], x00[...], upper, inverse, work, unit, u, x)


def refine_kernel(gram, rest, upper, inverse, out, up2, inv2, work, unit, u, x, second):
    up = upper[...]
    lo = up.T
    uh, u1, u2, u3 = slices(up, 0)
    lh, l1, l2, l3 = slices(lo, 1)
    left = jnp.concatenate([l2, l1, l1, l3, lh, l2, lh, l1, lh], axis=1)
    right = jnp.concatenate([u1, u2, u1, uh, u3, uh, u2, uh, u1], axis=0)
    resid = ((gram[...] - bf(lh, uh)) - bf(left, right)) + rest[...]
    first = inverse[...]
    one = jnp.where(eye(256), 1.0, 0.0)
    gap = mul(first, lo) - one
    e = mul_t(mul(first, resid), first) + mul_t(gap, gap)
    e = 0.5 * (e + e.T) + (gap + gap.T)
    second[...] = one + e
    size = jnp.sqrt(jnp.sum(e * e))

    @pl.when(size < 0.25)
    def _():
        y = one - low(e)
        for _ in range(2):
            f = mul_t(mul(y, e), y) + (mul_t(y, y) - one)
            y = y - mul(low(f), y)
        out[...] = mul(y, first)

    @pl.when(jnp.logical_not(size < 0.25))
    def _():
        work[...] = second[:128, :128]
        factor(work, unit, u, x)
        extend(second, u[...], x[...], up2, inv2, work, unit, u, x)
        out[...] = mul(inv2[...], first)


def front_kernel(flag, snap, test, sketch, sent, kept, th, tm, tl, s, e):
    step = pl.program_id(0)

    @pl.when(step == 0)
    def _():
        h, m, low_part = split(test[...])
        th[...], tm[...], tl[...] = h, m, low_part

    h, m, low_part = split(snap[...])
    block = (bf(low_part, th[...]) + bf(h, tl[...]) + bf(m, tm[...])) + (bf(m, th[...]) + bf(h, tm[...])) + bf(h, th[...])
    sketch[...] = block
    part = mul(block.T, block)

    @pl.when(step == 0)
    def _():
        s[...] = part
        e[...] = jnp.zeros_like(part)

    @pl.when(step > 0)
    def _():
        total, error = two_sum(s[...], part)
        s[...] = total
        e[...] += error

    @pl.when(step == pl.num_programs(0) - 1)
    def _():
        place_halves(flag, (s[...] + e[...]) * SCALE, sent, kept)


SCALE = 1.0 / 262144.0


def split(value):
    h = value.astype(BF16)
    m = value - h.astype(F32)
    mid = m.astype(BF16)
    return h, mid, (m - mid.astype(F32)).astype(BF16)


def two_sum(s, t):
    total = s + t
    part = total - s
    return total, (s - (total - part)) + (t - part)


def place_halves(flag, value, sent, kept):
    half = value.shape[0] // 2

    @pl.when(flag[0] == 0)
    def _():
        kept[...] = value[:half]
        sent[...] = value[half:]

    @pl.when(flag[0] != 0)
    def _():
        kept[...] = value[half:]
        sent[...] = value[:half]


def step_kernel(mode, flag, v, r, *outs):
    if mode == "plain":
        total = v[...] + r[...]
    elif mode == "first":
        total = jnp.concatenate(two_sum(v[...], r[...]), axis=1)
    else:
        n = v.shape[1] // 2
        total, error = two_sum(v[:, :n], r[:, :n])
        total = jnp.concatenate([total, error + (v[:, n:] + r[:, n:])], axis=1)
    if len(outs) == 1:
        outs[0][...] = total
    else:
        place_halves(flag, total, *outs)


def join_kernel(flag, v, r, out):
    half = v.shape[0]

    @pl.when(flag[0] == 0)
    def _():
        out[:half] = v[...]
        out[half:] = r[...]

    @pl.when(flag[0] != 0)
    def _():
        out[:half] = r[...]
        out[half:] = v[...]


VMEM = pl.BlockSpec(memory_space=pltpu.VMEM)
SMEM = pl.BlockSpec(memory_space=pltpu.SMEM)
LIMIT = 32 << 20


def square(*sizes):
    return [jax.ShapeDtypeStruct((n, n), F32) for n in sizes]


def scratch(*sizes):
    return [pltpu.VMEM((n, n), F32) for n in sizes]


def call(kernel, shapes, work, *args, flops=0):
    return pl.pallas_call(
        kernel,
        out_shape=shapes,
        in_specs=[SMEM if a.dtype == jnp.int32 else VMEM for a in args],
        out_specs=[VMEM] * len(shapes),
        scratch_shapes=work,
        compiler_params=pltpu.CompilerParams(vmem_limit_bytes=LIMIT),
        cost_estimate=pl.CostEstimate(flops=flops, bytes_accessed=sum(4 * a.size for a in args), transcendentals=0),
    )(*args)


def front(flag, snapshots, test):
    rows, depth = snapshots.shape
    rank = test.shape[1]
    block = rows // 4
    half = jax.ShapeDtypeStruct((rank // 2, rank), F32)
    parts = pl.BlockSpec((rank // 2, rank), lambda i: (0, 0))
    return pl.pallas_call(
        front_kernel,
        grid=(4,),
        out_shape=[jax.ShapeDtypeStruct((rows, rank), F32), half, half],
        in_specs=[SMEM, pl.BlockSpec((block, depth), lambda i: (i, 0)), pl.BlockSpec((depth, rank), lambda i: (0, 0))],
        out_specs=[pl.BlockSpec((block, rank), lambda i: (i, 0)), parts, parts],
        scratch_shapes=[pltpu.VMEM((depth, rank), BF16)] * 3 + scratch(rank, rank),
        compiler_params=pltpu.CompilerParams(vmem_limit_bytes=LIMIT),
        cost_estimate=pl.CostEstimate(flops=4 * 10**9, bytes_accessed=6 << 20, transcendentals=0),
    )(flag, snapshots, test)


def add_step(v, r, mode, flag=None):
    rows, width = v.shape
    width = 2 * width if mode == "first" else width
    shapes = [jax.ShapeDtypeStruct((rows, width), F32)] if flag is None else [jax.ShapeDtypeStruct((rows // 2, width), F32)] * 2
    out = call(functools.partial(step_kernel, mode), shapes, [], jnp.zeros((1,), jnp.int32) if flag is None else flag, v, r)
    return out[0] if flag is None else out


def join(value, perm, flag):
    rows, width = value.shape
    return call(join_kernel, [jax.ShapeDtypeStruct((2 * rows, width), F32)], [], flag, value, swap(value, perm))[0]


AXES = ("z", "x", "y", "core")


def pairs(change):
    def index(z, x, y, c):
        return ((z * 4 + x) * 4 + y) * 2 + c
    places = itertools.product(range(8), range(4), range(4), range(2))
    return [(index(*place), index(*change(*place))) for place in places]


CORE = pairs(lambda z, x, y, c: (z, x, y, c ^ 1))
A1 = pairs(lambda z, x, y, c: (z, x ^ 1, y, c) if c else (z, x, y ^ 1, c))
A2 = pairs(lambda z, x, y, c: (z, x ^ 3, y, c) if c else (z, x, y ^ 3, c))
B1 = pairs(lambda z, x, y, c: (z, x, y ^ 1, c) if c else (z, x ^ 1, y, c))
B2 = pairs(lambda z, x, y, c: (z, x, y ^ 3, c) if c else (z, x ^ 3, y, c))
Z1, Z2, Z3 = (pairs(lambda z, x, y, c, m=m: (z ^ m, x, y, c)) for m in (1, 3, 7))


def swap(value, perm):
    return lax.ppermute(value, AXES, perm)


def place():
    core, x, y = lax.axis_index("core"), lax.axis_index("x"), lax.axis_index("y")
    a, b = jnp.where(core == 1, x, y), jnp.where(core == 1, y, x)
    ring = ((a == 1) | (a == 2), a >= 2, (b == 1) | (b == 2), b >= 2)
    return [flag.astype(jnp.int32).reshape(1) for flag in (core, *ring)]


def after(value, *gates):
    return lax.optimization_barrier((value, *gates))[0]


def shards(snapshots, range_test, corange_test):
    core, a1, a2, b1, b2 = place()
    half = corange_test.shape[0] // 2
    others = lax.dynamic_slice_in_dim(corange_test, (1 - core[0]) * half, half)
    mine = lax.dynamic_slice_in_dim(corange_test, core[0] * half, half)

    sketch, sent, kept = front(core, snapshots, range_test)
    g0 = sent
    sent, kept = add_step(kept, swap(sent, CORE), "first", a1)
    g1 = sent
    recv = swap(sent, A1)
    out = jnp.dot(after(others, g0, g1), snapshots, precision=HIGHEST)
    sent, kept = add_step(kept, after(recv, out), "pair", a2)
    g2 = sent
    recv = swap(sent, A2)
    c_recv = swap(out, CORE)
    c_kept = jnp.dot(after(mine, g2), snapshots, precision=HIGHEST)
    value = add_step(kept, after(recv, c_kept), "pair")

    def corange_step(kept, recv, flag, gate):
        sent, kept = add_step(kept, after(recv, gate), "plain", flag)
        return sent, kept

    c_sent, c_kept = corange_step(c_kept, c_recv, a1, value)
    c_recv = swap(c_sent, A1)
    value = add_step(value, swap(value, B1), "pair")
    value = add_step(value, swap(value, B2), "pair")
    c_sent, c_kept = corange_step(c_kept, c_recv, a2, value)
    c_recv = swap(c_sent, A2)
    value = add_step(value, swap(value, Z1), "pair")
    c_sent, c_kept = corange_step(c_kept, c_recv, b1, value)
    c_recv = swap(c_sent, B1)
    value = add_step(value, swap(value, Z2), "pair")
    c_sent, c_kept = corange_step(c_kept, c_recv, b2, value)
    c_recv = swap(c_sent, B2)
    value = add_step(value, swap(value, Z3), "pair")
    c_value = add_step(c_kept, after(c_recv, value), "plain")
    c_recv = swap(c_value, Z1)
    value = join(value, A2, a2)
    c_value = add_step(c_value, after(c_recv, value), "plain")
    c_recv = swap(c_value, Z2)
    value = join(value, A1, a1)
    c_value = add_step(c_value, after(c_recv, value), "plain")
    c_recv = swap(c_value, Z3)
    value = join(value, CORE, core)

    n = value.shape[0]
    gram, rest = value[:, :n], value[:, n:]
    c_value = add_step(c_value, after(c_recv, gram), "plain")
    gram, c_value = lax.optimization_barrier((gram, c_value))
    c_value = join(c_value, B2, after(b2, gram))
    u00, x00 = call(factor_kernel, square(128, 128), scratch(128, 128), gram, flops=10**8)
    x00, c_value = lax.optimization_barrier((x00, c_value))
    c_value = join(c_value, B1, b1)
    upper, first = call(extend_kernel, square(n, n), scratch(128, 128, 128, 128), gram, u00, x00, flops=10**8)
    first, c_value = lax.optimization_barrier((first, c_value))
    c_value = join(c_value, A2, a2)
    inverse = call(refine_kernel, square(n), scratch(n, n, 128, 128, 128, 128, n), gram, rest, upper, first, flops=10**9)[0]
    inverse, c_value = lax.optimization_barrier((inverse, c_value))
    c_value = join(c_value, A1, a1)
    basis = jnp.einsum("rk,jk->rj", sketch, inverse, precision=HIGHEST)
    corange = join(c_value, CORE, core)
    crossed = jnp.dot(corange, range_test, precision=HIGHEST)
    core_out = jnp.einsum("jk,lk->jl", inverse, crossed, precision=HIGHEST)
    return basis, corange, core_out


def solution(mesh):
    fine = Mesh(mesh.devices.reshape(8, 4, 4, 2), AXES)
    in_specs = (P(AXES, None), P(), P(None, AXES))
    out_specs = (P(AXES, None), P(), P())
    return jax.shard_map(shards, mesh=fine, in_specs=in_specs, out_specs=out_specs, check_vma=False)
```

```python
import functools
import itertools

import jax
import jax.numpy as jnp
from jax import lax
from jax.experimental import pallas as pl
from jax.experimental.pallas import tpu as pltpu
from jax.sharding import Mesh, PartitionSpec as P

HIGHEST = lax.Precision.HIGHEST
F32, BF16 = jnp.float32, jnp.bfloat16


def mul(a, b):
    return lax.dot_general(a, b, (((1,), (0,)), ((), ())), precision=HIGHEST, preferred_element_type=F32)


def mul_t(a, b):
    return lax.dot_general(a, b, (((1,), (1,)), ((), ())), precision=HIGHEST, preferred_element_type=F32)


def factor(work, unit, upper, inverse):
    unit[...] = jnp.where(eye(128), 1.0, 0.0)
    for p in range(16):
        rows = pl.ds(8 * p, 8)
        panel, tail = work[rows, :], unit[rows, :]
        column = [jnp.broadcast_to(panel[:, 8 * p + j : 8 * p + j + 1], (8, 128)) for j in range(8)]
        s = [[column[j][i : i + 1, :] if j >= i else None for j in range(8)] for i in range(8)]
        r = [panel[i : i + 1, :] for i in range(8)]
        t = [tail[i : i + 1, :] for i in range(8)]
        inv = [None] * 8
        for j in range(8):
            inv[j] = 1.0 / s[j][j]
            for i in range(j + 1, 8):
                m = s[j][i] * inv[j]
                for k in range(i, 8):
                    s[i][k] = s[i][k] - m * s[j][k]
                r[i] = r[i] - m * r[j]
                t[i] = t[i] - m * t[j]
        for q in range(p + 1, 16):
            below = pl.ds(8 * q, 8)
            a, b = work[below, :], unit[below, :]
            c = [jnp.broadcast_to(a[:, 8 * p + j : 8 * p + j + 1], (8, 128)) for j in range(8)]
            for j in range(8):
                f = c[j] * inv[j]
                for k in range(j + 1, 8):
                    c[k] = c[k] - f * s[j][k]
                a = a - f * r[j]
                b = b - f * t[j]
            work[below, :] = a
            unit[below, :] = b
        root = [lax.rsqrt(s[i][i]) for i in range(8)]
        lane = lax.broadcasted_iota(jnp.int32, (1, 128), 1)
        upper[rows, :] = jnp.concatenate([jnp.where(lane >= 8 * p + i, r[i] * root[i], 0.0) for i in range(8)])
        inverse[rows, :] = jnp.concatenate([t[i] * root[i] for i in range(8)])


def eye(n):
    return lax.broadcasted_iota(jnp.int32, (n, n), 0) == lax.broadcasted_iota(jnp.int32, (n, n), 1)


def slices(value, axis):
    big = jnp.max(jnp.abs(value), axis=axis, keepdims=True) * 131072.0
    h = (value + big) - big
    m = value - h
    m1 = m.astype(BF16)
    m = m - m1.astype(F32)
    m2 = m.astype(BF16)
    m3 = (m - m2.astype(F32)).astype(BF16)
    return h.astype(BF16), m1, m2, m3


def extend(gram, u00, x00, upper, inverse, work, unit, u, x):
    u01 = mul(x00, gram[:128, 128:])
    upper[:128, :128] = u00
    upper[:128, 128:] = u01
    upper[128:, :128] = jnp.zeros((128, 128), F32)
    inverse[:128, :128] = x00
    inverse[:128, 128:] = jnp.zeros((128, 128), F32)
    l10 = u01.T
    work[...] = gram[128:, 128:] - mul(l10, u01)
    factor(work, unit, u, x)
    x11 = x[...]
    upper[128:, 128:] = u[...]
    inverse[128:, 128:] = x11
    inverse[128:, :128] = -mul(x11, mul(l10, x00))


def bf(a, b):
    return lax.dot_general(a, b, (((1,), (0,)), ((), ())), preferred_element_type=F32)


def low(e):
    row = lax.broadcasted_iota(jnp.int32, e.shape, 0)
    col = lax.broadcasted_iota(jnp.int32, e.shape, 1)
    return jnp.where(row > col, e, jnp.where(row == col, 0.5 * e, 0.0))


def factor_kernel(gram, u, x, work, unit):
    work[...] = gram[:128, :128]
    factor(work, unit, u, x)


def extend_kernel(gram, u00, x00, upper, inverse, work, unit, u, x):
    extend(gram, u00[...], x00[...], upper, inverse, work, unit, u, x)


def refine_kernel(gram, rest, upper, inverse, out, up2, inv2, work, unit, u, x, second):
    up = upper[...]
    lo = up.T
    uh, u1, u2, u3 = slices(up, 0)
    lh, l1, l2, l3 = slices(lo, 1)
    left = jnp.concatenate([l2, l1, l1, l3, lh, l2, lh, l1, lh], axis=1)
    right = jnp.concatenate([u1, u2, u1, uh, u3, uh, u2, uh, u1], axis=0)
    resid = ((gram[...] - bf(lh, uh)) - bf(left, right)) + rest[...]
    first = inverse[...]
    one = jnp.where(eye(256), 1.0, 0.0)
    gap = mul(first, lo) - one
    e = mul_t(mul(first, resid), first) + mul_t(gap, gap)
    e = 0.5 * (e + e.T) + (gap + gap.T)
    second[...] = one + e
    size = jnp.sqrt(jnp.sum(e * e))

    @pl.when(size < 0.25)
    def _():
        y = one - low(e)
        for _ in range(2):
            f = mul_t(mul(y, e), y) + (mul_t(y, y) - one)
            y = y - mul(low(f), y)
        out[...] = mul(y, first)

    @pl.when(jnp.logical_not(size < 0.25))
    def _():
        work[...] = second[:128, :128]
        factor(work, unit, u, x)
        extend(second, u[...], x[...], up2, inv2, work, unit, u, x)
        out[...] = mul(inv2[...], first)


def front_kernel(flag, snap, test, sketch, sent, kept, th, tm, tl, s, e):
    step = pl.program_id(0)

    @pl.when(step == 0)
    def _():
        h, m, low_part = split(test[...])
        th[...], tm[...], tl[...] = h, m, low_part

    h, m, low_part = split(snap[...])
    block = (bf(low_part, th[...]) + bf(h, tl[...]) + bf(m, tm[...])) + (bf(m, th[...]) + bf(h, tm[...])) + bf(h, th[...])
    sketch[...] = block
    part = mul(block.T, block)

    @pl.when(step == 0)
    def _():
        s[...] = part
        e[...] = jnp.zeros_like(part)

    @pl.when(step > 0)
    def _():
        total, error = two_sum(s[...], part)
        s[...] = total
        e[...] += error

    @pl.when(step == pl.num_programs(0) - 1)
    def _():
        place_halves(flag, (s[...] + e[...]) * SCALE, sent, kept)


SCALE = 1.0 / 262144.0


def split(value):
    h = value.astype(BF16)
    m = value - h.astype(F32)
    mid = m.astype(BF16)
    return h, mid, (m - mid.astype(F32)).astype(BF16)


def two_sum(s, t):
    total = s + t
    part = total - s
    return total, (s - (total - part)) + (t - part)


def place_halves(flag, value, sent, kept):
    half = value.shape[0] // 2

    @pl.when(flag[0] == 0)
    def _():
        kept[...] = value[:half]
        sent[...] = value[half:]

    @pl.when(flag[0] != 0)
    def _():
        kept[...] = value[half:]
        sent[...] = value[:half]


def step_kernel(mode, flag, v, r, *outs):
    if mode == "plain":
        total = v[...] + r[...]
    elif mode == "first":
        total = jnp.concatenate(two_sum(v[...], r[...]), axis=1)
    else:
        n = v.shape[1] // 2
        total, error = two_sum(v[:, :n], r[:, :n])
        total = jnp.concatenate([total, error + (v[:, n:] + r[:, n:])], axis=1)
    if len(outs) == 1:
        outs[0][...] = total
    else:
        place_halves(flag, total, *outs)


def pack(pair):
    half = pair.shape[0] // 2
    return jnp.concatenate([pair[:half], pair[half:]], axis=1)


def pack_kernel(v, r, out):
    n = v.shape[1] // 2
    total, error = two_sum(v[:, :n], r[:, :n])
    out[...] = pack(jnp.concatenate([total, error + (v[:, n:] + r[:, n:])], axis=1))


def add_packed(v, r):
    n = v.shape[1] // 4
    out = []
    for i in (0, 2):
        total, error = two_sum(v[:, i * n : i * n + n], r[:, i * n : i * n + n])
        rest = slice(i * n + n, i * n + 2 * n)
        out += [total, error + (v[:, rest] + r[:, rest])]
    return jnp.concatenate(out, axis=1)


def spread(flag, total, pair, sent, kept):
    half = total.shape[0] // 2
    place_halves(flag, total, sent.at[:half], kept.at[:half])
    sent[half:] = pair
    kept[half:] = pair


def open_kernel(flag, c, r, pair, sent, kept):
    spread(flag, c[...] + r[...], pair[...], sent, kept)


def merged_kernel(rows, flag, v, r, sent, kept):
    spread(flag, v[:rows] + r[:rows], add_packed(v[rows:], r[rows:]), sent, kept)


def double_kernel(rows, v, r, out):
    out[:rows] = v[:rows] + r[:rows]
    out[rows:] = add_packed(v[rows:], r[rows:])


def close_kernel(rows, v, r, c, pair):
    c[...] = v[:rows] + r[:rows]
    total = add_packed(v[rows:], r[rows:])
    half = total.shape[1] // 2
    pair[...] = jnp.concatenate([total[:, :half], total[:, half:]], axis=0)


def join_kernel(flag, v, r, out):
    half = v.shape[0]

    @pl.when(flag[0] == 0)
    def _():
        out[:half] = v[...]
        out[half:] = r[...]

    @pl.when(flag[0] != 0)
    def _():
        out[:half] = r[...]
        out[half:] = v[...]


VMEM = pl.BlockSpec(memory_space=pltpu.VMEM)
SMEM = pl.BlockSpec(memory_space=pltpu.SMEM)
LIMIT = 32 << 20


def square(*sizes):
    return [jax.ShapeDtypeStruct((n, n), F32) for n in sizes]


def scratch(*sizes):
    return [pltpu.VMEM((n, n), F32) for n in sizes]


def call(kernel, shapes, work, *args, flops=0):
    return pl.pallas_call(
        kernel,
        out_shape=shapes,
        in_specs=[SMEM if a.dtype == jnp.int32 else VMEM for a in args],
        out_specs=[VMEM] * len(shapes),
        scratch_shapes=work,
        compiler_params=pltpu.CompilerParams(vmem_limit_bytes=LIMIT),
        cost_estimate=pl.CostEstimate(flops=flops, bytes_accessed=sum(4 * a.size for a in args), transcendentals=0),
    )(*args)


def front(flag, snapshots, test):
    rows, depth = snapshots.shape
    rank = test.shape[1]
    block = rows // 4
    half = jax.ShapeDtypeStruct((rank // 2, rank), F32)
    parts = pl.BlockSpec((rank // 2, rank), lambda i: (0, 0))
    return pl.pallas_call(
        front_kernel,
        grid=(4,),
        out_shape=[jax.ShapeDtypeStruct((rows, rank), F32), half, half],
        in_specs=[SMEM, pl.BlockSpec((block, depth), lambda i: (i, 0)), pl.BlockSpec((depth, rank), lambda i: (0, 0))],
        out_specs=[pl.BlockSpec((block, rank), lambda i: (i, 0)), parts, parts],
        scratch_shapes=[pltpu.VMEM((depth, rank), BF16)] * 3 + scratch(rank, rank),
        compiler_params=pltpu.CompilerParams(vmem_limit_bytes=LIMIT),
        cost_estimate=pl.CostEstimate(flops=4 * 10**9, bytes_accessed=6 << 20, transcendentals=0),
    )(flag, snapshots, test)


def add_step(v, r, mode, flag=None):
    rows, width = v.shape
    width = 2 * width if mode == "first" else width
    shapes = [jax.ShapeDtypeStruct((rows, width), F32)] if flag is None else [jax.ShapeDtypeStruct((rows // 2, width), F32)] * 2
    out = call(functools.partial(step_kernel, mode), shapes, [], jnp.zeros((1,), jnp.int32) if flag is None else flag, v, r)
    return out[0] if flag is None else out


def join_halves(value, recv, flag):
    rows, width = value.shape
    return call(join_kernel, [jax.ShapeDtypeStruct((2 * rows, width), F32)], [], flag, value, recv)[0]


def join(value, perm, flag):
    return join_halves(value, swap(value, perm), flag)


AXES = ("z", "x", "y", "core")


def pairs(change):
    def index(z, x, y, c):
        return ((z * 4 + x) * 4 + y) * 2 + c
    places = itertools.product(range(8), range(4), range(4), range(2))
    return [(index(*place), index(*change(*place))) for place in places]


CORE = pairs(lambda z, x, y, c: (z, x, y, c ^ 1))
A1, A2 = (pairs(lambda z, x, y, c, m=m: (z, x ^ m, y, c) if c else (z, x, y ^ m, c)) for m in (1, 3))
WALKS = zip("xxzzz", (1, 3, 1, 3, 7), "zzzyy", (1, 3, 7, 1, 3))


def walk(axis, mask, place):
    return tuple(p ^ mask if name == axis else p for name, p in zip("zxyc", place))


B1, B2, B3, B4, B5 = (
    pairs(lambda *p, w=w: walk(w[2], w[3], p) if p[3] else walk(w[0], w[1], p)) for w in WALKS
)


def swap(value, perm):
    return lax.ppermute(value, AXES, perm)


def place():
    core, x, y, z = (lax.axis_index(name) for name in ("core", "x", "y", "z"))
    a = jnp.where(core == 1, x, y)
    gray = z ^ (z >> 1)
    b1 = jnp.where(core == 1, gray & 1, (x ^ (x >> 1)) & 1)
    b2 = jnp.where(core == 1, (gray >> 1) & 1, x >> 1)
    return [flag.astype(jnp.int32).reshape(1) for flag in (core, (a ^ (a >> 1)) & 1, a >> 1, b1, b2)]


def after(value, *gates):
    return lax.optimization_barrier((value, *gates))[0]


def shards(snapshots, range_test, corange_test):
    core, a1, a2, b1, b2 = place()
    half = corange_test.shape[0] // 2
    others = lax.dynamic_slice_in_dim(corange_test, (1 - core[0]) * half, half)
    mine = lax.dynamic_slice_in_dim(corange_test, core[0] * half, half)

    sketch, sent, kept = front(core, snapshots, range_test)
    g0 = sent
    sent, kept = add_step(kept, swap(sent, CORE), "first", a1)
    g1 = sent
    recv = swap(sent, A1)
    out = jnp.dot(after(others, g0, g1), snapshots, precision=HIGHEST)
    sent, kept = add_step(kept, after(recv, out), "pair", a2)
    g2 = sent
    recv = swap(sent, A2)
    c_recv = swap(out, CORE)
    c_kept = jnp.dot(after(mine, g2), snapshots, precision=HIGHEST)
    n = kept.shape[1] // 2
    rows = [jax.ShapeDtypeStruct((r, 4 * n), F32) for r in (48, 48, 32, 32)]
    pair = call(pack_kernel, [jax.ShapeDtypeStruct((16, 4 * n), F32)], [], kept, after(recv, c_kept))[0]
    c_sent, c_kept = add_step(c_kept, c_recv, "plain", a1)
    c_sent, c_kept = add_step(c_kept, swap(c_sent, A1), "plain", a2)
    v_sent, v_kept = call(open_kernel, rows[:2], [], b1, c_kept, swap(c_sent, A2), pair)
    v_sent, v_kept = call(functools.partial(merged_kernel, 32), rows[2:], [], b2, v_kept, swap(v_sent, B1))
    value = call(functools.partial(double_kernel, 16), rows[3:], [], v_kept, swap(v_sent, B2))[0]
    for perm in (B3, B4):
        value = call(functools.partial(double_kernel, 16), rows[3:], [], value, swap(value, perm))[0]
    shapes = [jax.ShapeDtypeStruct((16, 4 * n), F32), jax.ShapeDtypeStruct((32, 2 * n), F32)]
    c_value, value = call(functools.partial(close_kernel, 16), shapes, [], value, swap(value, B5))

    value, c_value = join(value, A2, a2), join(c_value, B2, b2)
    value, c_value = lax.optimization_barrier((value, c_value))
    value, c_value = join(value, A1, a1), join(c_value, B1, b1)
    value, c_value = lax.optimization_barrier((value, c_value))
    recv = swap(c_value, A2)
    value = join(value, CORE, core)
    gram, rest = value[:, :n], value[:, n:]

    u00, x00 = call(factor_kernel, square(128, 128), scratch(128, 128), gram, flops=10**8)
    c_value = join_halves(c_value, after(recv, x00), a2)
    x00, c_value = lax.optimization_barrier((x00, c_value))
    recv = swap(c_value, A1)
    upper, first = call(extend_kernel, square(n, n), scratch(128, 128, 128, 128), gram, u00, x00, flops=10**8)
    inverse = call(refine_kernel, square(n), scratch(n, n, 128, 128, 128, 128, n), gram, rest, upper, first, flops=10**9)[0]
    c_value = join_halves(c_value, after(recv, inverse), a1)
    inverse, c_value = lax.optimization_barrier((inverse, c_value))
    recv = swap(c_value, CORE)
    basis = jnp.einsum("rk,jk->rj", sketch, inverse, precision=HIGHEST)
    own = jnp.dot(c_value, range_test, precision=HIGHEST)
    recv = after(recv, own, basis)
    corange = join_halves(c_value, recv, core)
    other = jnp.dot(recv, range_test, precision=HIGHEST)
    crossed = join_halves(own, other, core)
    core_out = jnp.einsum("jk,lk->jl", inverse, crossed, precision=HIGHEST)
    return basis, corange, core_out


def solution(mesh):
    fine = Mesh(mesh.devices.reshape(8, 4, 4, 2), AXES)
    in_specs = (P(AXES, None), P(), P(None, AXES))
    out_specs = (P(AXES, None), P(), P())
    return jax.shard_map(shards, mesh=fine, in_specs=in_specs, out_specs=out_specs, check_vma=False)
```

```python
import functools
import itertools

import jax
import jax.numpy as jnp
from jax import lax
from jax.experimental import pallas as pl
from jax.experimental.pallas import tpu as pltpu
from jax.sharding import Mesh, PartitionSpec as P

HIGHEST = lax.Precision.HIGHEST
F32, BF16 = jnp.float32, jnp.bfloat16


def mul(a, b):
    return lax.dot_general(a, b, (((1,), (0,)), ((), ())), precision=HIGHEST, preferred_element_type=F32)


def mul_t(a, b):
    return lax.dot_general(a, b, (((1,), (1,)), ((), ())), precision=HIGHEST, preferred_element_type=F32)


def factor(work, unit, upper, inverse):
    unit[...] = jnp.where(eye(128), 1.0, 0.0)
    for p in range(16):
        rows = pl.ds(8 * p, 8)
        panel, tail = work[rows, :], unit[rows, :]
        column = [jnp.broadcast_to(panel[:, 8 * p + j : 8 * p + j + 1], (8, 128)) for j in range(8)]
        s = [[column[j][i : i + 1, :] if j >= i else None for j in range(8)] for i in range(8)]
        r = [panel[i : i + 1, :] for i in range(8)]
        t = [tail[i : i + 1, :] for i in range(8)]
        inv = [None] * 8
        for j in range(8):
            inv[j] = 1.0 / s[j][j]
            for i in range(j + 1, 8):
                m = s[j][i] * inv[j]
                for k in range(i, 8):
                    s[i][k] = s[i][k] - m * s[j][k]
                r[i] = r[i] - m * r[j]
                t[i] = t[i] - m * t[j]
        for q in range(p + 1, 16):
            below = pl.ds(8 * q, 8)
            a, b = work[below, :], unit[below, :]
            c = [jnp.broadcast_to(a[:, 8 * p + j : 8 * p + j + 1], (8, 128)) for j in range(8)]
            for j in range(8):
                f = c[j] * inv[j]
                for k in range(j + 1, 8):
                    c[k] = c[k] - f * s[j][k]
                a = a - f * r[j]
                b = b - f * t[j]
            work[below, :] = a
            unit[below, :] = b
        root = [lax.rsqrt(s[i][i]) for i in range(8)]
        lane = lax.broadcasted_iota(jnp.int32, (1, 128), 1)
        upper[rows, :] = jnp.concatenate([jnp.where(lane >= 8 * p + i, r[i] * root[i], 0.0) for i in range(8)])
        inverse[rows, :] = jnp.concatenate([t[i] * root[i] for i in range(8)])


def eye(n):
    return lax.broadcasted_iota(jnp.int32, (n, n), 0) == lax.broadcasted_iota(jnp.int32, (n, n), 1)


def slices(value, axis):
    big = jnp.max(jnp.abs(value), axis=axis, keepdims=True) * 131072.0
    h = (value + big) - big
    m = value - h
    m1 = m.astype(BF16)
    m = m - m1.astype(F32)
    m2 = m.astype(BF16)
    m3 = (m - m2.astype(F32)).astype(BF16)
    return h.astype(BF16), m1, m2, m3


def extend(gram, u00, x00, upper, inverse, work, unit, u, x):
    u01 = mul(x00, gram[:128, 128:])
    upper[:128, :128] = u00
    upper[:128, 128:] = u01
    upper[128:, :128] = jnp.zeros((128, 128), F32)
    inverse[:128, :128] = x00
    inverse[:128, 128:] = jnp.zeros((128, 128), F32)
    l10 = u01.T
    work[...] = gram[128:, 128:] - mul(l10, u01)
    factor(work, unit, u, x)
    x11 = x[...]
    upper[128:, 128:] = u[...]
    inverse[128:, 128:] = x11
    inverse[128:, :128] = -mul(x11, mul(l10, x00))


def bf(a, b):
    return lax.dot_general(a, b, (((1,), (0,)), ((), ())), preferred_element_type=F32)


def low(e):
    row = lax.broadcasted_iota(jnp.int32, e.shape, 0)
    col = lax.broadcasted_iota(jnp.int32, e.shape, 1)
    return jnp.where(row > col, e, jnp.where(row == col, 0.5 * e, 0.0))


def factor_kernel(gram, u, x, work, unit):
    work[...] = gram[:128, :128]
    factor(work, unit, u, x)


def extend_kernel(gram, u00, x00, upper, inverse, work, unit, u, x):
    extend(gram, u00[...], x00[...], upper, inverse, work, unit, u, x)


def refine_kernel(gram, rest, upper, inverse, out, up2, inv2, work, unit, u, x, second):
    up = upper[...]
    lo = up.T
    uh, u1, u2, u3 = slices(up, 0)
    lh, l1, l2, l3 = slices(lo, 1)
    left = jnp.concatenate([l2, l1, l1, l3, lh, l2, lh, l1, lh], axis=1)
    right = jnp.concatenate([u1, u2, u1, uh, u3, uh, u2, uh, u1], axis=0)
    resid = ((gram[...] - bf(lh, uh)) - bf(left, right)) + rest[...]
    first = inverse[...]
    one = jnp.where(eye(256), 1.0, 0.0)
    gap = mul(first, lo) - one
    e = mul_t(mul(first, resid), first) + mul_t(gap, gap)
    e = 0.5 * (e + e.T) + (gap + gap.T)
    second[...] = one + e
    size = jnp.sqrt(jnp.sum(e * e))

    @pl.when(size < 0.25)
    def _():
        y = one - low(e)
        for _ in range(2):
            f = mul_t(mul(y, e), y) + (mul_t(y, y) - one)
            y = y - mul(low(f), y)
        out[...] = mul(y, first)

    @pl.when(jnp.logical_not(size < 0.25))
    def _():
        work[...] = second[:128, :128]
        factor(work, unit, u, x)
        extend(second, u[...], x[...], up2, inv2, work, unit, u, x)
        out[...] = mul(inv2[...], first)


def front_kernel(flag, snap, test, sketch, sent, kept, th, tm, tl, s, e):
    step = pl.program_id(0)

    @pl.when(step == 0)
    def _():
        h, m, low_part = split(test[...])
        th[...], tm[...], tl[...] = h, m, low_part

    h, m, low_part = split(snap[...])
    block = (bf(low_part, th[...]) + bf(h, tl[...]) + bf(m, tm[...])) + (bf(m, th[...]) + bf(h, tm[...])) + bf(h, th[...])
    sketch[...] = block
    part = mul(block.T, block)

    @pl.when(step == 0)
    def _():
        s[...] = part
        e[...] = jnp.zeros_like(part)

    @pl.when(step > 0)
    def _():
        total, error = two_sum(s[...], part)
        s[...] = total
        e[...] += error

    @pl.when(step == pl.num_programs(0) - 1)
    def _():
        place_halves(flag, (s[...] + e[...]) * SCALE, sent, kept)


SCALE = 1.0 / 262144.0


def split(value):
    h = value.astype(BF16)
    m = value - h.astype(F32)
    mid = m.astype(BF16)
    return h, mid, (m - mid.astype(F32)).astype(BF16)


def two_sum(s, t):
    total = s + t
    part = total - s
    return total, (s - (total - part)) + (t - part)


def place_halves(flag, value, sent, kept):
    half = value.shape[0] // 2

    @pl.when(flag[0] == 0)
    def _():
        kept[...] = value[:half]
        sent[...] = value[half:]

    @pl.when(flag[0] != 0)
    def _():
        kept[...] = value[half:]
        sent[...] = value[:half]


def pack(pair):
    half = pair.shape[0] // 2
    return jnp.concatenate([pair[:half], pair[half:]], axis=1)


def pack_kernel(v, r, out):
    n = v.shape[1] // 2
    total, error = two_sum(v[:, :n], r[:, :n])
    out[...] = pack(jnp.concatenate([total, error + (v[:, n:] + r[:, n:])], axis=1))


def add_packed(v, r):
    n = v.shape[1] // 4
    out = []
    for i in (0, 2):
        total, error = two_sum(v[:, i * n : i * n + n], r[:, i * n : i * n + n])
        rest = slice(i * n + n, i * n + 2 * n)
        out += [total, error + (v[:, rest] + r[:, rest])]
    return jnp.concatenate(out, axis=1)


def scatter(place, total, outs, pair=None):
    rows = total.shape[0] // 4
    for m, out in enumerate(outs):
        part = pl.ds(pl.multiple_of((place[0] ^ m) * rows, 8), rows)
        out[:rows] = total[part, :]
        if pair is not None:
            out[rows:] = pair


def fold(add, v, r1, r2, r3):
    return add(add(v, r1), add(r2, r3))


def add_pair(v, r):
    n = v.shape[1] // 2
    total, error = two_sum(v[:, :n], r[:, :n])
    return jnp.concatenate([total, error + (v[:, n:] + r[:, n:])], axis=1)


def first_kernel(place, v, r, *outs):
    total = outs[4]
    total[...] = jnp.concatenate(two_sum(v[...], r[...]), axis=1)
    scatter(place, total, outs[:4])


def plain_kernel(place, v, r, *outs):
    total = outs[4]
    total[...] = v[...] + r[...]
    scatter(place, total, outs[:4])


def pack_kernel(v, r1, r2, r3, out):
    out[...] = pack(fold(add_pair, v[...], r1[...], r2[...], r3[...]))


def open_kernel(place, v, r1, r2, r3, pair, *outs):
    total = outs[4]
    total[...] = (v[...] + r1[...]) + (r2[...] + r3[...])
    scatter(place, total, outs[:4], pair[...])


def fold_kernel(v, r1, r2, r3, out):
    rows = v.shape[0] // 2
    top, bottom = [ref[:rows] for ref in (v, r1, r2, r3)], [ref[rows:] for ref in (v, r1, r2, r3)]
    out[:rows] = fold(jnp.add, *top)
    out[rows:] = fold(add_packed, *bottom)


def double_kernel(v, r, out):
    rows = v.shape[0] // 2
    out[:rows] = v[:rows] + r[:rows]
    out[rows:] = add_packed(v[rows:], r[rows:])


def close_kernel(v, r1, r2, r3, c, pair):
    rows = v.shape[0] // 2
    top, bottom = [ref[:rows] for ref in (v, r1, r2, r3)], [ref[rows:] for ref in (v, r1, r2, r3)]
    c[...] = fold(jnp.add, *top)
    total = fold(add_packed, *bottom)
    half = total.shape[1] // 2
    pair[...] = jnp.concatenate([total[:, :half], total[:, half:]], axis=0)


def gather_kernel(place, v, r1, r2, r3, out):
    rows = v.shape[0]
    for m, ref in enumerate((v, r1, r2, r3)):
        out[pl.ds(pl.multiple_of((place[0] ^ m) * rows, 8), rows), :] = ref[...]


def join_kernel(flag, v, r, out):
    half = v.shape[0]

    @pl.when(flag[0] == 0)
    def _():
        out[:half] = v[...]
        out[half:] = r[...]

    @pl.when(flag[0] != 0)
    def _():
        out[:half] = r[...]
        out[half:] = v[...]


VMEM = pl.BlockSpec(memory_space=pltpu.VMEM)
SMEM = pl.BlockSpec(memory_space=pltpu.SMEM)
LIMIT = 32 << 20


def square(*sizes):
    return [jax.ShapeDtypeStruct((n, n), F32) for n in sizes]


def scratch(*sizes):
    return [pltpu.VMEM((n, n), F32) for n in sizes]


def call(kernel, shapes, work, *args, flops=0):
    return pl.pallas_call(
        kernel,
        out_shape=shapes,
        in_specs=[SMEM if a.dtype == jnp.int32 else VMEM for a in args],
        out_specs=[VMEM] * len(shapes),
        scratch_shapes=work,
        compiler_params=pltpu.CompilerParams(vmem_limit_bytes=LIMIT),
        cost_estimate=pl.CostEstimate(flops=flops, bytes_accessed=sum(4 * a.size for a in args), transcendentals=0),
    )(*args)


def front(flag, snapshots, test):
    rows, depth = snapshots.shape
    rank = test.shape[1]
    block = rows // 4
    half = jax.ShapeDtypeStruct((rank // 2, rank), F32)
    parts = pl.BlockSpec((rank // 2, rank), lambda i: (0, 0))
    return pl.pallas_call(
        front_kernel,
        grid=(4,),
        out_shape=[jax.ShapeDtypeStruct((rows, rank), F32), half, half],
        in_specs=[SMEM, pl.BlockSpec((block, depth), lambda i: (i, 0)), pl.BlockSpec((depth, rank), lambda i: (0, 0))],
        out_specs=[pl.BlockSpec((block, rank), lambda i: (i, 0)), parts, parts],
        scratch_shapes=[pltpu.VMEM((depth, rank), BF16)] * 3 + scratch(rank, rank),
        compiler_params=pltpu.CompilerParams(vmem_limit_bytes=58 << 20),
        cost_estimate=pl.CostEstimate(flops=4 * 10**9, bytes_accessed=6 << 20, transcendentals=0),
    )(flag, snapshots, test)


def join_halves(value, recv, flag):
    rows, width = value.shape
    return call(join_kernel, [jax.ShapeDtypeStruct((2 * rows, width), F32)], [], flag, value, recv)[0]


AXES = ("z", "x", "y", "core")


def pairs(change):
    def index(z, x, y, c):
        return ((z * 4 + x) * 4 + y) * 2 + c
    places = itertools.product(range(8), range(4), range(4), range(2))
    return [(index(*place), index(*change(*place))) for place in places]


CORE = pairs(lambda z, x, y, c: (z, x, y, c ^ 1))
RING = (1, 3, 2)
A = [pairs(lambda z, x, y, c, m=m: (z, x ^ m, y, c) if c else (z, x, y ^ m, c)) for m in RING]
B = [pairs(lambda z, x, y, c, m=m: (z ^ m, x, y, c) if c else (z, x ^ m, y, c)) for m in RING]
HALF = pairs(lambda z, x, y, c: (z ^ 7, x, y, c))
D = [pairs(lambda z, x, y, c, m=m: (z, x, y ^ m, c) if c else (z ^ m, x, y, c)) for m in RING]


def swap(value, perm):
    return lax.ppermute(value, AXES, perm)


def gather(place, value, received):
    rows, width = value.shape
    return call(gather_kernel, [jax.ShapeDtypeStruct((4 * rows, width), F32)], [], place, value, *received)[0]


def sheets(count, rows, width):
    return [jax.ShapeDtypeStruct((rows, width), F32)] * count


def place():
    core, x, y, z = (lax.axis_index(name) for name in ("core", "x", "y", "z"))
    a, b = jnp.where(core == 1, x, y), jnp.where(core == 1, z, x)
    return [flag.astype(jnp.int32).reshape(1) for flag in (core, a ^ (a >> 1), (b ^ (b >> 1)) & 3)]


def after(value, *gates):
    return lax.optimization_barrier((value, *gates))[0]


def shards(snapshots, range_test, corange_test):
    core, a, b = place()
    half = corange_test.shape[0] // 2
    others = lax.dynamic_slice_in_dim(corange_test, (1 - core[0]) * half, half)
    mine = lax.dynamic_slice_in_dim(corange_test, core[0] * half, half)

    sketch, sent, kept = front(core, snapshots, range_test)
    g0 = sent
    n, wide = sent.shape[1], snapshots.shape[1]
    kept, *sent = call(first_kernel, sheets(4, 32, 2 * n), [pltpu.VMEM((128, 2 * n), F32)], a, kept, swap(sent, CORE))
    recv = [swap(part, perm) for part, perm in zip(sent, A)]
    c_sent = jnp.dot(after(others, *sent), snapshots, precision=HIGHEST)
    c_recv = swap(c_sent, CORE)
    c_kept = jnp.dot(after(mine, c_sent), snapshots, precision=HIGHEST)
    recv = [after(part, c_kept) for part in recv]
    pair = call(pack_kernel, sheets(1, 16, wide), [], kept, *recv)[0]
    c_kept, *c_sent = call(plain_kernel, sheets(4, 64, wide), [pltpu.VMEM((256, wide), F32)], a, c_kept, c_recv)
    c_recv = [swap(part, perm) for part, perm in zip(c_sent, A)]
    kept, *sent = call(open_kernel, sheets(4, 32, wide), [pltpu.VMEM((64, wide), F32)], b, c_kept, *c_recv, pair)
    recv = [swap(part, perm) for part, perm in zip(sent, B)]
    value = call(fold_kernel, sheets(1, 32, wide), [], kept, *recv)[0]
    value = call(double_kernel, sheets(1, 32, wide), [], value, swap(value, HALF))[0]
    recv = [swap(value, perm) for perm in D]
    c_value, value = call(close_kernel, sheets(1, 16, wide) + sheets(1, 32, 2 * n), [], value, *recv)

    value = gather(a, value, [swap(value, perm) for perm in A])
    value, c_value = lax.optimization_barrier((value, c_value))
    recv, c_recv = swap(value, CORE), [swap(c_value, perm) for perm in B]
    value = join_halves(value, recv, core)
    gram, rest = value[:, :n], value[:, n:]

    u00, x00 = call(factor_kernel, square(128, 128), scratch(128, 128), gram, flops=10**8)
    c_value = gather(b, c_value, [after(part, x00) for part in c_recv])
    x00, c_value = lax.optimization_barrier((x00, c_value))
    c_recv = [swap(c_value, perm) for perm in A]
    upper, first = call(extend_kernel, square(n, n), scratch(128, 128, 128, 128), gram, u00, x00, flops=10**8)
    inverse = call(refine_kernel, square(n), scratch(n, n, 128, 128, 128, 128, n), gram, rest, upper, first, flops=10**9)[0]
    c_value = gather(a, c_value, [after(part, inverse) for part in c_recv])
    inverse, c_value = lax.optimization_barrier((inverse, c_value))
    recv = swap(c_value, CORE)
    basis = jnp.einsum("rk,jk->rj", sketch, inverse, precision=HIGHEST)
    own = jnp.dot(c_value, range_test, precision=HIGHEST)
    recv = after(recv, own, basis)
    corange = join_halves(c_value, recv, core)
    other = jnp.dot(recv, range_test, precision=HIGHEST)
    crossed = join_halves(own, other, core)
    core_out = jnp.einsum("jk,lk->jl", inverse, crossed, precision=HIGHEST)
    return basis, corange, core_out


def solution(mesh):
    fine = Mesh(mesh.devices.reshape(8, 4, 4, 2), AXES)
    in_specs = (P(AXES, None), P(), P(None, AXES))
    out_specs = (P(AXES, None), P(), P())
    return jax.shard_map(shards, mesh=fine, in_specs=in_specs, out_specs=out_specs, check_vma=False)
```

```python
import functools
import itertools

import jax
import jax.numpy as jnp
from jax import lax
from jax.experimental import pallas as pl
from jax.experimental.pallas import tpu as pltpu
from jax.sharding import Mesh, PartitionSpec as P

HIGHEST = lax.Precision.HIGHEST
F32, BF16 = jnp.float32, jnp.bfloat16


def mul(a, b):
    return lax.dot_general(a, b, (((1,), (0,)), ((), ())), precision=HIGHEST, preferred_element_type=F32)


def mul_t(a, b):
    return lax.dot_general(a, b, (((1,), (1,)), ((), ())), precision=HIGHEST, preferred_element_type=F32)


def factor(work, unit, upper, inverse):
    unit[...] = jnp.where(eye(128), 1.0, 0.0)
    for p in range(16):
        rows = pl.ds(8 * p, 8)
        panel, tail = work[rows, :], unit[rows, :]
        column = [jnp.broadcast_to(panel[:, 8 * p + j : 8 * p + j + 1], (8, 128)) for j in range(8)]
        s = [[column[j][i : i + 1, :] if j >= i else None for j in range(8)] for i in range(8)]
        r = [panel[i : i + 1, :] for i in range(8)]
        t = [tail[i : i + 1, :] for i in range(8)]
        inv = [None] * 8
        for j in range(8):
            inv[j] = 1.0 / s[j][j]
            for i in range(j + 1, 8):
                m = s[j][i] * inv[j]
                for k in range(i, 8):
                    s[i][k] = s[i][k] - m * s[j][k]
                r[i] = r[i] - m * r[j]
                t[i] = t[i] - m * t[j]
        for q in range(p + 1, 16):
            below = pl.ds(8 * q, 8)
            a, b = work[below, :], unit[below, :]
            c = [jnp.broadcast_to(a[:, 8 * p + j : 8 * p + j + 1], (8, 128)) for j in range(8)]
            for j in range(8):
                f = c[j] * inv[j]
                for k in range(j + 1, 8):
                    c[k] = c[k] - f * s[j][k]
                a = a - f * r[j]
                b = b - f * t[j]
            work[below, :] = a
            unit[below, :] = b
        root = [lax.rsqrt(s[i][i]) for i in range(8)]
        lane = lax.broadcasted_iota(jnp.int32, (1, 128), 1)
        upper[rows, :] = jnp.concatenate([jnp.where(lane >= 8 * p + i, r[i] * root[i], 0.0) for i in range(8)])
        inverse[rows, :] = jnp.concatenate([t[i] * root[i] for i in range(8)])


def eye(n):
    return lax.broadcasted_iota(jnp.int32, (n, n), 0) == lax.broadcasted_iota(jnp.int32, (n, n), 1)


def slices(value, axis):
    big = jnp.max(jnp.abs(value), axis=axis, keepdims=True) * 131072.0
    h = (value + big) - big
    m = value - h
    m1 = m.astype(BF16)
    m = m - m1.astype(F32)
    m2 = m.astype(BF16)
    m3 = (m - m2.astype(F32)).astype(BF16)
    return h.astype(BF16), m1, m2, m3


def extend(gram, u00, x00, upper, inverse, work, unit, u, x):
    u01 = mul(x00, gram[:128, 128:])
    upper[:128, :128] = u00
    upper[:128, 128:] = u01
    upper[128:, :128] = jnp.zeros((128, 128), F32)
    inverse[:128, :128] = x00
    inverse[:128, 128:] = jnp.zeros((128, 128), F32)
    l10 = u01.T
    work[...] = gram[128:, 128:] - mul(l10, u01)
    factor(work, unit, u, x)
    x11 = x[...]
    upper[128:, 128:] = u[...]
    inverse[128:, 128:] = x11
    inverse[128:, :128] = -mul(x11, mul(l10, x00))


def bf(a, b):
    return lax.dot_general(a, b, (((1,), (0,)), ((), ())), preferred_element_type=F32)


def bf_t(a, b):
    return lax.dot_general(a, b, (((0,), (0,)), ((), ())), preferred_element_type=F32)


def low(e):
    row = lax.broadcasted_iota(jnp.int32, e.shape, 0)
    col = lax.broadcasted_iota(jnp.int32, e.shape, 1)
    return jnp.where(row > col, e, jnp.where(row == col, 0.5 * e, 0.0))


def factor_kernel(gram, u, x, work, unit):
    work[...] = gram[:128, :128]
    factor(work, unit, u, x)


def extend_kernel(gram, u00, x00, upper, inverse, work, unit, u, x):
    extend(gram, u00[...], x00[...], upper, inverse, work, unit, u, x)


def refine_kernel(gram, rest, upper, inverse, out, up2, inv2, work, unit, u, x, second):
    up = upper[...]
    lo = up.T
    uh, u1, u2, u3 = slices(up, 0)
    lh, l1, l2, l3 = slices(lo, 1)
    left = jnp.concatenate([l2, l1, l1, l3, lh, l2, lh, l1, lh], axis=1)
    right = jnp.concatenate([u1, u2, u1, uh, u3, uh, u2, uh, u1], axis=0)
    resid = ((gram[...] - bf(lh, uh)) - bf(left, right)) + rest[...]
    first = inverse[...]
    one = jnp.where(eye(256), 1.0, 0.0)
    gap = mul(first, lo) - one
    e = mul_t(mul(first, resid), first) + mul_t(gap, gap)
    e = 0.5 * (e + e.T) + (gap + gap.T)
    second[...] = one + e
    size = jnp.sqrt(jnp.sum(e * e))

    @pl.when(size < 0.06)
    def _():
        y = one - low(e)
        f = mul_t(mul(y, e), y) + (mul_t(y, y) - one)
        y = y - mul(low(f), y)
        out[...] = mul(y, first)

    @pl.when(jnp.logical_not(size < 0.06))
    def _():
        work[...] = second[:128, :128]
        factor(work, unit, u, x)
        extend(second, u[...], x[...], up2, inv2, work, unit, u, x)
        out[...] = mul(inv2[...], first)


def front_kernel(flag, snap, test, sketch, sent, kept, th, tm, tl, s, e):
    step = pl.program_id(0)

    @pl.when(step == 0)
    def _():
        h, m, low_part = split(test[...])
        th[...], tm[...], tl[...] = h, m, low_part

    h, m, low_part = split(snap[...])
    block = (bf(low_part, th[...]) + bf(h, tl[...]) + bf(m, tm[...])) + (bf(m, th[...]) + bf(h, tm[...])) + bf(h, th[...])
    sketch[...] = block
    h, m, low_part = split(block)
    cross = bf_t(h, m) + bf_t(h, low_part)
    part = (bf_t(m, m) + (cross + cross.T)) + bf_t(h, h)

    @pl.when(step == 0)
    def _():
        s[...] = part
        e[...] = jnp.zeros_like(part)

    @pl.when(step > 0)
    def _():
        total, error = two_sum(s[...], part)
        s[...] = total
        e[...] += error

    @pl.when(step == pl.num_programs(0) - 1)
    def _():
        place_halves(flag, (s[...] + e[...]) * SCALE, sent, kept)


SCALE = 1.0 / 262144.0


def split(value):
    h = value.astype(BF16)
    m = value - h.astype(F32)
    mid = m.astype(BF16)
    return h, mid, (m - mid.astype(F32)).astype(BF16)


def two_sum(s, t):
    total = s + t
    part = total - s
    return total, (s - (total - part)) + (t - part)


def place_halves(flag, value, sent, kept):
    half = value.shape[0] // 2

    @pl.when(flag[0] == 0)
    def _():
        kept[...] = value[:half]
        sent[...] = value[half:]

    @pl.when(flag[0] != 0)
    def _():
        kept[...] = value[half:]
        sent[...] = value[:half]


def add_packed(v, r):
    n = v.shape[1] // 4
    out = []
    for i in (0, 2):
        total, error = two_sum(v[:, i * n : i * n + n], r[:, i * n : i * n + n])
        rest = slice(i * n + n, i * n + 2 * n)
        out += [total, error + (v[:, rest] + r[:, rest])]
    return jnp.concatenate(out, axis=1)


def scatter(place, total, outs, pair):
    rows = total.shape[0] // 4
    for m, out in enumerate(outs):
        out[:rows] = total[pl.ds(pl.multiple_of((place[0] ^ m) * rows, 8), rows), :]
        out[rows:] = pair


def fold(add, v, r1, r2, r3):
    return add(add(v, r1), add(r2, r3))


def start_kernel(place, g, g_recv, c, c_recv, *outs):
    *outs, pairs_in, total = outs
    pairs_in[...] = jnp.concatenate(two_sum(g[...], g_recv[...]), axis=1)
    total[...] = c[...] + c_recv[...]
    rows, depth, width = total.shape[0] // 4, pairs_in.shape[0] // 8, pairs_in.shape[1]
    for m, out in enumerate(outs):
        at = place[0] ^ m
        out[:rows] = total[pl.ds(pl.multiple_of(at * rows, 8), rows), :]
        for i in (0, 1):
            part = pl.ds(pl.multiple_of((2 * at + i) * depth, 8), depth)
            out[rows:, i * width : (i + 1) * width] = pairs_in[part, :]


def open_kernel(place, v, r1, r2, r3, *outs):
    total = outs[4]
    rows = total.shape[0]
    top, bottom = [ref[:rows] for ref in (v, r1, r2, r3)], [ref[rows:] for ref in (v, r1, r2, r3)]
    total[...] = fold(jnp.add, *top)
    scatter(place, total, outs[:4], fold(add_packed, *bottom))


def fold_kernel(v, r1, r2, r3, out):
    rows = v.shape[0] // 2
    top, bottom = [ref[:rows] for ref in (v, r1, r2, r3)], [ref[rows:] for ref in (v, r1, r2, r3)]
    out[:rows] = fold(jnp.add, *top)
    out[rows:] = fold(add_packed, *bottom)


def double_kernel(v, r, out):
    rows = v.shape[0] // 2
    out[:rows] = v[:rows] + r[:rows]
    out[rows:] = add_packed(v[rows:], r[rows:])


def close_kernel(v, r1, r2, r3, c, pair):
    rows = v.shape[0] // 2
    top, bottom = [ref[:rows] for ref in (v, r1, r2, r3)], [ref[rows:] for ref in (v, r1, r2, r3)]
    c[...] = fold(jnp.add, *top)
    total = fold(add_packed, *bottom)
    half = total.shape[1] // 2
    pair[...] = jnp.concatenate([total[:, :half], total[:, half:]], axis=0)


def gather_kernel(place, v, r1, r2, r3, out):
    rows = v.shape[0]
    for m, ref in enumerate((v, r1, r2, r3)):
        out[pl.ds(pl.multiple_of((place[0] ^ m) * rows, 8), rows), :] = ref[...]


def join_kernel(flag, v, r, out):
    half = v.shape[0]

    @pl.when(flag[0] == 0)
    def _():
        out[:half] = v[...]
        out[half:] = r[...]

    @pl.when(flag[0] != 0)
    def _():
        out[:half] = r[...]
        out[half:] = v[...]


VMEM = pl.BlockSpec(memory_space=pltpu.VMEM)
SMEM = pl.BlockSpec(memory_space=pltpu.SMEM)
LIMIT = 32 << 20


def square(*sizes):
    return [jax.ShapeDtypeStruct((n, n), F32) for n in sizes]


def scratch(*sizes):
    return [pltpu.VMEM((n, n), F32) for n in sizes]


def call(kernel, shapes, work, *args, flops=0):
    return pl.pallas_call(
        kernel,
        out_shape=shapes,
        in_specs=[SMEM if a.dtype == jnp.int32 else VMEM for a in args],
        out_specs=[VMEM] * len(shapes),
        scratch_shapes=work,
        compiler_params=pltpu.CompilerParams(vmem_limit_bytes=LIMIT),
        cost_estimate=pl.CostEstimate(flops=flops, bytes_accessed=sum(4 * a.size for a in args), transcendentals=0),
    )(*args)


def front(flag, snapshots, test):
    rows, depth = snapshots.shape
    rank = test.shape[1]
    block = rows // 2
    half = jax.ShapeDtypeStruct((rank // 2, rank), F32)
    parts = pl.BlockSpec((rank // 2, rank), lambda i: (0, 0))
    return pl.pallas_call(
        front_kernel,
        grid=(2,),
        out_shape=[jax.ShapeDtypeStruct((rows, rank), F32), half, half],
        in_specs=[SMEM, pl.BlockSpec((block, depth), lambda i: (i, 0)), pl.BlockSpec((depth, rank), lambda i: (0, 0))],
        out_specs=[pl.BlockSpec((block, rank), lambda i: (i, 0)), parts, parts],
        scratch_shapes=[pltpu.VMEM((depth, rank), BF16)] * 3 + scratch(rank, rank),
        compiler_params=pltpu.CompilerParams(vmem_limit_bytes=58 << 20),
        cost_estimate=pl.CostEstimate(flops=4 * 10**9, bytes_accessed=6 << 20, transcendentals=0),
    )(flag, snapshots, test)


def join_halves(value, recv, flag):
    rows, width = value.shape
    return call(join_kernel, [jax.ShapeDtypeStruct((2 * rows, width), F32)], [], flag, value, recv)[0]


AXES = ("z", "x", "y", "core")


def pairs(change):
    def index(z, x, y, c):
        return ((z * 4 + x) * 4 + y) * 2 + c
    places = itertools.product(range(8), range(4), range(4), range(2))
    return [(index(*place), index(*change(*place))) for place in places]


CORE = pairs(lambda z, x, y, c: (z, x, y, c ^ 1))
RING = (1, 3, 2)
A = [pairs(lambda z, x, y, c, m=m: (z, x ^ m, y, c) if c else (z, x, y ^ m, c)) for m in RING]
B = [pairs(lambda z, x, y, c, m=m: (z ^ m, x, y, c) if c else (z, x ^ m, y, c)) for m in RING]
HALF = pairs(lambda z, x, y, c: (z ^ 7, x, y, c))
D = [pairs(lambda z, x, y, c, m=m: (z, x, y ^ m, c) if c else (z ^ m, x, y, c)) for m in RING]


def swap(value, perm):
    return lax.ppermute(value, AXES, perm)


def gather(place, value, received):
    rows, width = value.shape
    return call(gather_kernel, [jax.ShapeDtypeStruct((4 * rows, width), F32)], [], place, value, *received)[0]


def sheets(count, rows, width):
    return [jax.ShapeDtypeStruct((rows, width), F32)] * count


def place():
    core, x, y, z = (lax.axis_index(name) for name in ("core", "x", "y", "z"))
    a, b = jnp.where(core == 1, x, y), jnp.where(core == 1, z, x)
    return [flag.astype(jnp.int32).reshape(1) for flag in (core, a ^ (a >> 1), (b ^ (b >> 1)) & 3)]


def after(value, *gates):
    return lax.optimization_barrier((value, *gates))[0]


def shards(snapshots, range_test, corange_test):
    core, a, b = place()
    half = corange_test.shape[0] // 2
    others = lax.dynamic_slice_in_dim(corange_test, (1 - core[0]) * half, half)
    mine = lax.dynamic_slice_in_dim(corange_test, core[0] * half, half)

    sketch, sent, kept = front(core, snapshots, range_test)
    n, wide = sent.shape[1], snapshots.shape[1]
    recv = swap(sent, CORE)
    c_sent = jnp.dot(after(others, sent), snapshots, precision=HIGHEST)
    c_recv = swap(c_sent, CORE)
    c_kept = jnp.dot(after(mine, c_sent), snapshots, precision=HIGHEST)
    work = [pltpu.VMEM((128, 2 * n), F32), pltpu.VMEM((256, wide), F32)]
    kept, *sent = call(start_kernel, sheets(4, 80, wide), work, a, kept, recv, c_kept, c_recv)
    recv = [swap(part, perm) for part, perm in zip(sent, A)]
    kept, *sent = call(open_kernel, sheets(4, 32, wide), [pltpu.VMEM((64, wide), F32)], b, kept, *recv)
    recv = [swap(part, perm) for part, perm in zip(sent, B)]
    value = call(fold_kernel, sheets(1, 32, wide), [], kept, *recv)[0]
    value = call(double_kernel, sheets(1, 32, wide), [], value, swap(value, HALF))[0]
    recv = [swap(value, perm) for perm in D]
    c_value, value = call(close_kernel, sheets(1, 16, wide) + sheets(1, 32, 2 * n), [], value, *recv)

    value = gather(a, value, [swap(value, perm) for perm in A])
    value, c_value = lax.optimization_barrier((value, c_value))
    recv, c_recv = swap(value, CORE), [swap(c_value, perm) for perm in B]
    value = join_halves(value, recv, core)
    gram, rest = value[:, :n], value[:, n:]

    u00, x00 = call(factor_kernel, square(128, 128), scratch(128, 128), gram, flops=10**8)
    c_value = gather(b, c_value, [after(part, x00) for part in c_recv])
    x00, c_value = lax.optimization_barrier((x00, c_value))
    c_recv = [swap(c_value, perm) for perm in A]
    upper, first = call(extend_kernel, square(n, n), scratch(128, 128, 128, 128), gram, u00, x00, flops=10**8)
    inverse = call(refine_kernel, square(n), scratch(n, n, 128, 128, 128, 128, n), gram, rest, upper, first, flops=10**9)[0]
    c_value = gather(a, c_value, [after(part, inverse) for part in c_recv])
    inverse, c_value = lax.optimization_barrier((inverse, c_value))
    recv = swap(c_value, CORE)
    basis = jnp.einsum("rk,jk->rj", sketch, inverse, precision=HIGHEST)
    own = jnp.dot(c_value, range_test, precision=HIGHEST)
    recv = after(recv, own, basis)
    corange = join_halves(c_value, recv, core)
    other = jnp.dot(recv, range_test, precision=HIGHEST)
    crossed = join_halves(own, other, core)
    core_out = jnp.einsum("jk,lk->jl", inverse, crossed, precision=HIGHEST)
    return basis, corange, core_out


def solution(mesh):
    fine = Mesh(mesh.devices.reshape(8, 4, 4, 2), AXES)
    in_specs = (P(AXES, None), P(), P(None, AXES))
    out_specs = (P(AXES, None), P(), P())
    return jax.shard_map(shards, mesh=fine, in_specs=in_specs, out_specs=out_specs, check_vma=False)
```

```python
import functools
import itertools

import jax
import jax.numpy as jnp
from jax import lax
from jax.experimental import pallas as pl
from jax.experimental.pallas import tpu as pltpu
from jax.sharding import Mesh, PartitionSpec as P

HIGHEST = lax.Precision.HIGHEST
F32, BF16 = jnp.float32, jnp.bfloat16


def mul(a, b):
    return lax.dot_general(a, b, (((1,), (0,)), ((), ())), precision=HIGHEST, preferred_element_type=F32)


def mul_t(a, b):
    return lax.dot_general(a, b, (((1,), (1,)), ((), ())), precision=HIGHEST, preferred_element_type=F32)


def factor(work, unit, upper, inverse):
    unit[...] = jnp.where(eye(128), 1.0, 0.0)
    for p in range(16):
        rows = pl.ds(8 * p, 8)
        panel, tail = work[rows, :], unit[rows, :]
        column = [jnp.broadcast_to(panel[:, 8 * p + j : 8 * p + j + 1], (8, 128)) for j in range(8)]
        s = [[column[j][i : i + 1, :] if j >= i else None for j in range(8)] for i in range(8)]
        r = [panel[i : i + 1, :] for i in range(8)]
        t = [tail[i : i + 1, :] for i in range(8)]
        inv = [None] * 8
        for j in range(8):
            inv[j] = 1.0 / s[j][j]
            for i in range(j + 1, 8):
                m = s[j][i] * inv[j]
                for k in range(i, 8):
                    s[i][k] = s[i][k] - m * s[j][k]
                r[i] = r[i] - m * r[j]
                t[i] = t[i] - m * t[j]
        for q in range(p + 1, 16):
            below = pl.ds(8 * q, 8)
            a, b = work[below, :], unit[below, :]
            c = [jnp.broadcast_to(a[:, 8 * p + j : 8 * p + j + 1], (8, 128)) for j in range(8)]
            for j in range(8):
                f = c[j] * inv[j]
                for k in range(j + 1, 8):
                    c[k] = c[k] - f * s[j][k]
                a = a - f * r[j]
                b = b - f * t[j]
            work[below, :] = a
            unit[below, :] = b
        root = [lax.rsqrt(s[i][i]) for i in range(8)]
        lane = lax.broadcasted_iota(jnp.int32, (1, 128), 1)
        upper[rows, :] = jnp.concatenate([jnp.where(lane >= 8 * p + i, r[i] * root[i], 0.0) for i in range(8)])
        inverse[rows, :] = jnp.concatenate([t[i] * root[i] for i in range(8)])


def eye(n):
    return lax.broadcasted_iota(jnp.int32, (n, n), 0) == lax.broadcasted_iota(jnp.int32, (n, n), 1)


def slices(value, axis):
    big = jnp.max(jnp.abs(value), axis=axis, keepdims=True) * 131072.0
    h = (value + big) - big
    m = value - h
    m1 = m.astype(BF16)
    m = m - m1.astype(F32)
    m2 = m.astype(BF16)
    m3 = (m - m2.astype(F32)).astype(BF16)
    return h.astype(BF16), m1, m2, m3


def extend(gram, u00, x00, upper, inverse, work, unit, u, x):
    u01 = mul(x00, gram[:128, 128:])
    upper[:128, :128] = u00
    upper[:128, 128:] = u01
    upper[128:, :128] = jnp.zeros((128, 128), F32)
    inverse[:128, :128] = x00
    inverse[:128, 128:] = jnp.zeros((128, 128), F32)
    l10 = u01.T
    work[...] = gram[128:, 128:] - mul(l10, u01)
    factor(work, unit, u, x)
    x11 = x[...]
    upper[128:, 128:] = u[...]
    inverse[128:, 128:] = x11
    inverse[128:, :128] = -mul(x11, mul(l10, x00))


def bf(a, b):
    return lax.dot_general(a, b, (((1,), (0,)), ((), ())), preferred_element_type=F32)


def bf_t(a, b):
    return lax.dot_general(a, b, (((0,), (0,)), ((), ())), preferred_element_type=F32)


def low(e):
    row = lax.broadcasted_iota(jnp.int32, e.shape, 0)
    col = lax.broadcasted_iota(jnp.int32, e.shape, 1)
    return jnp.where(row > col, e, jnp.where(row == col, 0.5 * e, 0.0))


def factor_kernel(gram, u, x, work, unit):
    work[...] = gram[:128, :128]
    factor(work, unit, u, x)


def extend_kernel(gram, u00, x00, upper, inverse, work, unit, u, x):
    extend(gram, u00[...], x00[...], upper, inverse, work, unit, u, x)


def refine_kernel(gram, rest, upper, inverse, out, up2, inv2, work, unit, u, x, second):
    up = upper[...]
    lo = up.T
    uh, u1, u2, u3 = slices(up, 0)
    lh, l1, l2, l3 = slices(lo, 1)
    left = jnp.concatenate([l2, l1, l1, l3, lh, l2, lh, l1, lh], axis=1)
    right = jnp.concatenate([u1, u2, u1, uh, u3, uh, u2, uh, u1], axis=0)
    resid = ((gram[...] - bf(lh, uh)) - bf(left, right)) + rest[...]
    first = inverse[...]
    one = jnp.where(eye(256), 1.0, 0.0)
    gap = mul(first, lo) - one
    e = mul_t(mul(first, resid), first) + mul_t(gap, gap)
    e = 0.5 * (e + e.T) + (gap + gap.T)
    second[...] = one + e
    size = jnp.sqrt(jnp.sum(e * e))

    @pl.when(size < 0.25)
    def _():
        y = one - low(e)
        for _ in range(2):
            f = mul_t(mul(y, e), y) + (mul_t(y, y) - one)
            y = y - mul(low(f), y)
        out[...] = mul(y, first)

    @pl.when(jnp.logical_not(size < 0.25))
    def _():
        work[...] = second[:128, :128]
        factor(work, unit, u, x)
        extend(second, u[...], x[...], up2, inv2, work, unit, u, x)
        out[...] = mul(inv2[...], first)


def front_kernel(flag, snap, test, sketch, sent, kept, th, tm, tl, s, e):
    step = pl.program_id(0)

    @pl.when(step == 0)
    def _():
        h, m, low_part = split(test[...])
        th[...], tm[...], tl[...] = h, m, low_part

    h, m, low_part = split(snap[...])
    block = (bf(low_part, th[...]) + bf(h, tl[...]) + bf(m, tm[...])) + (bf(m, th[...]) + bf(h, tm[...])) + bf(h, th[...])
    sketch[...] = block
    h, m, low_part = split(block)
    cross = bf_t(h, m) + bf_t(h, low_part)
    part = (bf_t(m, m) + (cross + cross.T)) + bf_t(h, h)

    @pl.when(step == 0)
    def _():
        s[...] = part
        e[...] = jnp.zeros_like(part)

    @pl.when(step > 0)
    def _():
        total, error = two_sum(s[...], part)
        s[...] = total
        e[...] += error

    @pl.when(step == pl.num_programs(0) - 1)
    def _():
        place_halves(flag, (s[...] + e[...]) * SCALE, sent, kept)


SCALE = 1.0 / 262144.0


def split(value):
    h = value.astype(BF16)
    m = value - h.astype(F32)
    mid = m.astype(BF16)
    return h, mid, (m - mid.astype(F32)).astype(BF16)


def two_sum(s, t):
    total = s + t
    part = total - s
    return total, (s - (total - part)) + (t - part)


def place_halves(flag, value, sent, kept):
    half = value.shape[0] // 2

    @pl.when(flag[0] == 0)
    def _():
        kept[...] = value[:half]
        sent[...] = value[half:]

    @pl.when(flag[0] != 0)
    def _():
        kept[...] = value[half:]
        sent[...] = value[:half]


def add_packed(v, r):
    n = v.shape[1] // 4
    out = []
    for i in (0, 2):
        total, error = two_sum(v[:, i * n : i * n + n], r[:, i * n : i * n + n])
        rest = slice(i * n + n, i * n + 2 * n)
        out += [total, error + (v[:, rest] + r[:, rest])]
    return jnp.concatenate(out, axis=1)


def scatter(place, total, outs, pair):
    rows = total.shape[0] // 4
    for m, out in enumerate(outs):
        out[:rows] = total[pl.ds(pl.multiple_of((place[0] ^ m) * rows, 8), rows), :]
        out[rows:] = pair


def fold(add, v, r1, r2, r3):
    return add(add(v, r1), add(r2, r3))


def start_kernel(place, g, g_recv, c, c_recv, *outs):
    *outs, pairs_in, total = outs
    pairs_in[...] = jnp.concatenate(two_sum(g[...], g_recv[...]), axis=1)
    total[...] = c[...] + c_recv[...]
    rows, depth, width = total.shape[0] // 4, pairs_in.shape[0] // 8, pairs_in.shape[1]
    for m, out in enumerate(outs):
        at = place[0] ^ m
        out[:rows] = total[pl.ds(pl.multiple_of(at * rows, 8), rows), :]
        for i in (0, 1):
            part = pl.ds(pl.multiple_of((2 * at + i) * depth, 8), depth)
            out[rows:, i * width : (i + 1) * width] = pairs_in[part, :]


def open_kernel(place, v, r1, r2, r3, *outs):
    total = outs[4]
    rows = total.shape[0]
    top, bottom = [ref[:rows] for ref in (v, r1, r2, r3)], [ref[rows:] for ref in (v, r1, r2, r3)]
    total[...] = fold(jnp.add, *top)
    scatter(place, total, outs[:4], fold(add_packed, *bottom))


def fold_kernel(v, r1, r2, r3, out):
    rows = v.shape[0] // 2
    top, bottom = [ref[:rows] for ref in (v, r1, r2, r3)], [ref[rows:] for ref in (v, r1, r2, r3)]
    out[:rows] = fold(jnp.add, *top)
    out[rows:] = fold(add_packed, *bottom)


def double_kernel(v, r, out):
    rows = v.shape[0] // 2
    out[:rows] = v[:rows] + r[:rows]
    out[rows:] = add_packed(v[rows:], r[rows:])


def close_kernel(v, r1, r2, r3, c, pair):
    rows = v.shape[0] // 2
    top, bottom = [ref[:rows] for ref in (v, r1, r2, r3)], [ref[rows:] for ref in (v, r1, r2, r3)]
    c[...] = fold(jnp.add, *top)
    total = fold(add_packed, *bottom)
    half = total.shape[1] // 2
    pair[...] = jnp.concatenate([total[:, :half], total[:, half:]], axis=0)


def gather_kernel(place, v, r1, r2, r3, out):
    rows = v.shape[0]
    for m, ref in enumerate((v, r1, r2, r3)):
        out[pl.ds(pl.multiple_of((place[0] ^ m) * rows, 8), rows), :] = ref[...]


def join_kernel(flag, v, r, out):
    half = v.shape[0]

    @pl.when(flag[0] == 0)
    def _():
        out[:half] = v[...]
        out[half:] = r[...]

    @pl.when(flag[0] != 0)
    def _():
        out[:half] = r[...]
        out[half:] = v[...]


VMEM = pl.BlockSpec(memory_space=pltpu.VMEM)
SMEM = pl.BlockSpec(memory_space=pltpu.SMEM)
LIMIT = 32 << 20


def square(*sizes):
    return [jax.ShapeDtypeStruct((n, n), F32) for n in sizes]


def scratch(*sizes):
    return [pltpu.VMEM((n, n), F32) for n in sizes]


def call(kernel, shapes, work, *args, flops=0):
    return pl.pallas_call(
        kernel,
        out_shape=shapes,
        in_specs=[SMEM if a.dtype == jnp.int32 else VMEM for a in args],
        out_specs=[VMEM] * len(shapes),
        scratch_shapes=work,
        compiler_params=pltpu.CompilerParams(vmem_limit_bytes=LIMIT),
        cost_estimate=pl.CostEstimate(flops=flops, bytes_accessed=sum(4 * a.size for a in args), transcendentals=0),
    )(*args)


def front(flag, snapshots, test):
    rows, depth = snapshots.shape
    rank = test.shape[1]
    block = rows // 2
    half = jax.ShapeDtypeStruct((rank // 2, rank), F32)
    parts = pl.BlockSpec((rank // 2, rank), lambda i: (0, 0))
    return pl.pallas_call(
        front_kernel,
        grid=(2,),
        out_shape=[jax.ShapeDtypeStruct((rows, rank), F32), half, half],
        in_specs=[SMEM, pl.BlockSpec((block, depth), lambda i: (i, 0)), pl.BlockSpec((depth, rank), lambda i: (0, 0))],
        out_specs=[pl.BlockSpec((block, rank), lambda i: (i, 0)), parts, parts],
        scratch_shapes=[pltpu.VMEM((depth, rank), BF16)] * 3 + scratch(rank, rank),
        compiler_params=pltpu.CompilerParams(vmem_limit_bytes=58 << 20),
        cost_estimate=pl.CostEstimate(flops=4 * 10**9, bytes_accessed=6 << 20, transcendentals=0),
    )(flag, snapshots, test)


def join_halves(value, recv, flag):
    rows, width = value.shape
    return call(join_kernel, [jax.ShapeDtypeStruct((2 * rows, width), F32)], [], flag, value, recv)[0]


AXES = ("z", "x", "y", "core")


def pairs(change):
    def index(z, x, y, c):
        return ((z * 4 + x) * 4 + y) * 2 + c
    places = itertools.product(range(8), range(4), range(4), range(2))
    return [(index(*place), index(*change(*place))) for place in places]


CORE = pairs(lambda z, x, y, c: (z, x, y, c ^ 1))
RING = (1, 3, 2)
A = [pairs(lambda z, x, y, c, m=m: (z, x ^ m, y, c) if c else (z, x, y ^ m, c)) for m in RING]
B = [pairs(lambda z, x, y, c, m=m: (z ^ m, x, y, c) if c else (z, x ^ m, y, c)) for m in RING]
HALF = pairs(lambda z, x, y, c: (z ^ 7, x, y, c))
D = [pairs(lambda z, x, y, c, m=m: (z, x, y ^ m, c) if c else (z ^ m, x, y, c)) for m in RING]


def swap(value, perm):
    return lax.ppermute(value, AXES, perm)


def gather(place, value, received):
    rows, width = value.shape
    return call(gather_kernel, [jax.ShapeDtypeStruct((4 * rows, width), F32)], [], place, value, *received)[0]


def sheets(count, rows, width):
    return [jax.ShapeDtypeStruct((rows, width), F32)] * count


def place():
    core, x, y, z = (lax.axis_index(name) for name in ("core", "x", "y", "z"))
    a, b = jnp.where(core == 1, x, y), jnp.where(core == 1, z, x)
    return [flag.astype(jnp.int32).reshape(1) for flag in (core, a ^ (a >> 1), (b ^ (b >> 1)) & 3)]


def after(value, *gates):
    return lax.optimization_barrier((value, *gates))[0]


def shards(snapshots, range_test, corange_test):
    core, a, b = place()
    half = corange_test.shape[0] // 2
    others = lax.dynamic_slice_in_dim(corange_test, (1 - core[0]) * half, half)
    mine = lax.dynamic_slice_in_dim(corange_test, core[0] * half, half)

    sketch, sent, kept = front(core, snapshots, range_test)
    n, wide = sent.shape[1], snapshots.shape[1]
    recv = swap(sent, CORE)
    c_sent = jnp.dot(after(others, recv), snapshots, precision=HIGHEST)
    c_recv = swap(c_sent, CORE)
    c_kept = jnp.dot(after(mine, c_sent), snapshots, precision=HIGHEST)
    work = [pltpu.VMEM((128, 2 * n), F32), pltpu.VMEM((256, wide), F32)]
    kept, *sent = call(start_kernel, sheets(4, 80, wide), work, a, kept, recv, c_kept, c_recv)
    recv = [swap(part, perm) for part, perm in zip(sent, A)]
    kept, *sent = call(open_kernel, sheets(4, 32, wide), [pltpu.VMEM((64, wide), F32)], b, kept, *recv)
    recv = [swap(part, perm) for part, perm in zip(sent, B)]
    value = call(fold_kernel, sheets(1, 32, wide), [], kept, *recv)[0]
    value = call(double_kernel, sheets(1, 32, wide), [], value, swap(value, HALF))[0]
    recv = [swap(value, perm) for perm in D]
    c_value, value = call(close_kernel, sheets(1, 16, wide) + sheets(1, 32, 2 * n), [], value, *recv)

    value = gather(a, value, [swap(value, perm) for perm in A])
    value, c_value = lax.optimization_barrier((value, c_value))
    recv, c_recv = swap(value, CORE), [swap(c_value, perm) for perm in B]
    value = join_halves(value, recv, core)
    gram, rest = value[:, :n], value[:, n:]

    u00, x00 = call(factor_kernel, square(128, 128), scratch(128, 128), gram, flops=10**8)
    c_value = gather(b, c_value, [after(part, x00) for part in c_recv])
    x00, c_value = lax.optimization_barrier((x00, c_value))
    c_recv = [swap(c_value, perm) for perm in A]
    upper, first = call(extend_kernel, square(n, n), scratch(128, 128, 128, 128), gram, u00, x00, flops=10**8)
    inverse = call(refine_kernel, square(n), scratch(n, n, 128, 128, 128, 128, n), gram, rest, upper, first, flops=10**9)[0]
    c_value = gather(a, c_value, [after(part, inverse) for part in c_recv])
    inverse, c_value = lax.optimization_barrier((inverse, c_value))
    recv = swap(c_value, CORE)
    basis = jnp.einsum("rk,jk->rj", sketch, inverse, precision=HIGHEST)
    own = jnp.dot(c_value, range_test, precision=HIGHEST)
    recv = after(recv, own, basis)
    corange = join_halves(c_value, recv, core)
    other = jnp.dot(recv, range_test, precision=HIGHEST)
    crossed = join_halves(own, other, core)
    core_out = jnp.einsum("jk,lk->jl", inverse, crossed, precision=HIGHEST)
    return basis, corange, core_out


def solution(mesh):
    fine = Mesh(mesh.devices.reshape(8, 4, 4, 2), AXES)
    in_specs = (P(AXES, None), P(), P(None, AXES))
    out_specs = (P(AXES, None), P(), P())
    return jax.shard_map(shards, mesh=fine, in_specs=in_specs, out_specs=out_specs, check_vma=False)
```
